32 devices in a mesh: dp: 16 (over z, x, core), fsdp: 2 (over y).
Axes of the slice: x: 2, y: 2, z: 4, core: 2. Of those that a mesh axis runs over, the one named last changes fastest.
Arguments:
- inputs: bfloat16 [32, 2048, 768], P('dp', 'fsdp'), may hold values from -6 to 6
- cotangent: bfloat16 [32, 2048, 768], P('dp', 'fsdp'), may hold values from -6 to 6
- lengths: int32 [32], P('dp'), may hold values from 512 to 2048, as said below
- w_query: float32 [768, 768], P(None, ('dp', 'fsdp')), may hold values from -0.0546875 to 0.0546875
- w_key: float32 [768, 768], P(None, ('dp', 'fsdp')), may hold values from -0.21875 to 0.21875
- w_value: float32 [768, 768], P(None, ('dp', 'fsdp')), may hold values from -0.21875 to 0.21875
- w_out: float32 [768, 768], P(None, ('dp', 'fsdp')), may hold values from -0.875 to 0.875
- w_gate: float32 [768, 2048], P(None, ('dp', 'fsdp')), may hold values from -0.21875 to 0.21875
- w_up: float32 [768, 2048], P(None, ('dp', 'fsdp')), may hold values from -0.21875 to 0.21875
- w_down: float32 [2048, 768], P(None, ('dp', 'fsdp')), may hold values from -0.125 to 0.125
- gain_attn: float32 [768], P(('dp', 'fsdp')), may hold values from 0.5 to 1.5
- gain_ffn: float32 [768], P(('dp', 'fsdp')), may hold values from 0.5 to 1.5
- bias_table: float32 [32, 12], replicated, may hold values from -3 to 3
Outputs:
- output: float32 [32, 2048, 768], P('dp', 'fsdp')
- grad_inputs: float32 [32, 2048, 768], P('dp', 'fsdp')
- grad_w_query: float32 [768, 768], P(None, ('dp', 'fsdp'))
- grad_w_key: float32 [768, 768], P(None, ('dp', 'fsdp'))
- grad_w_value: float32 [768, 768], P(None, ('dp', 'fsdp'))
- grad_w_out: float32 [768, 768], P(None, ('dp', 'fsdp'))
- grad_w_gate: float32 [768, 2048], P(None, ('dp', 'fsdp'))
- grad_w_up: float32 [768, 2048], P(None, ('dp', 'fsdp'))
- grad_w_down: float32 [2048, 768], P(None, ('dp', 'fsdp'))
- grad_gain_attn: float32 [768], P(('dp', 'fsdp'))
- grad_gain_ffn: float32 [768], P(('dp', 'fsdp'))
- grad_bias_table: float32 [32, 12], replicated
The draws below stay inside these ranges and needn't reach their ends.
Inputs may be any that keep to these rules, and one draw needn't show every extreme that they name: `lengths`: each entry counts the valid tokens of one sequence, which fill the start of its slot of 2048; the first sequence fills its whole slot and the second has the least length.
All inputs are finite; a program needn't handle non-finite values.
Results may differ from the reference program's by a relative error of at most 0.015.
The reference program's roundings to bfloat16 on the way count: a program that leaves them out, or rounds other values in their place, can miss the bound.
Values may be sent and summed in bfloat16 or wider, within the bound.
No kernel may reach another device: no remote copies, remote signals or barrier semaphores. Data moves between devices by JAX's collectives and lax.ppermute only.
A program may use at most 320 MiB of HBM per device.

```python
import jax
import jax.numpy as jnp
from jax import lax

D = 768
HEADS = 12
HEAD_DIM = 64
FF = 2048
BUCKETS = 32
SLOT = 2048
SEQS = 32


def draw_lengths(key, part):
    drawn = jax.random.randint(key, (SEQS,), SLOT // 4, SLOT + 1, dtype=jnp.int32)
    drawn = drawn.at[0].set(SLOT)
    return drawn.at[1].set(SLOT // 4)


def raised(result, rng, source, target, shards_of, factor):
    def block_of(position):
        return (jnp.arange(result.shape[position]) // (result.shape[position] // shards_of)).reshape((-1,) + (1,) * (result.ndim - 1 - position))

    near = jax.random.permutation(rng, shards_of)[block_of(target)]
    other_side = (block_of(target) + shards_of // 2) % shards_of
    return jnp.where((block_of(source) == near) | (block_of(source) == other_side), factor * result, result)


def steps_of(stream_key, shape, shards, low, top_value):
    gain, own = 1.0, jax.random.fold_in(stream_key, 6)
    for axis_at, parts in shards:
        draws = jnp.exp(jax.random.uniform(jax.random.fold_in(own, axis_at), (parts,), jnp.float32, low / len(shards), top_value / len(shards)))
        gain = gain * jnp.repeat(draws, shape[axis_at] // parts).reshape([-1 if axis == axis_at else 1 for axis in range(len(shape))])
    return gain


def gaussian(stream_key, shape, width, limit, pieces=(), held_as=jnp.bfloat16):
    array = jax.random.normal(stream_key, shape, jnp.float32) * width
    if len(pieces) > 0:
        array = steps_of(stream_key, shape, pieces, -0.22, 0.18) * array
    return jnp.clip(array, min=-limit, max=limit).astype(held_as)


def heavy_noise(key, shape, scale, most, split, heavy, kind=jnp.bfloat16):
    entries = scale * jax.random.normal(key, shape, jnp.float32)
    if split:
        entries = entries * steps_of(key, shape, split, -0.22, 0.18)
    return jnp.clip(raised(entries, jax.random.fold_in(key, 3), *heavy), -most, most).astype(kind)


def setup_inputs(seed: int = 0) -> dict:
    arg_keys = jax.random.split(jax.random.key(seed), 14)
    inputs = gaussian(arg_keys[0], (SEQS, SLOT, D), 1.0, 6.0, ((0, 16), (1, 2)))
    cotangent = heavy_noise(arg_keys[1], (SEQS, SLOT, D), 1.0, 6.0, ((0, 16), (1, 2)), (0, 2, 16, 2.0))
    lengths = draw_lengths(jax.random.fold_in(arg_keys[13], 71), 0)
    w_query = gaussian(arg_keys[3], (D, D), (D * 16) ** -0.5, 0.0546875, ((1, 32),), jnp.float32)
    w_key = gaussian(arg_keys[4], (D, D), D ** -0.5, 0.21875, ((1, 32),), jnp.float32)
    w_value = gaussian(arg_keys[5], (D, D), D ** -0.5, 0.21875, ((1, 32),), jnp.float32)
    w_out = gaussian(arg_keys[6], (D, D), (D // 16) ** -0.5, 0.875, ((1, 32),), jnp.float32)
    w_gate = gaussian(arg_keys[7], (D, FF), D ** -0.5, 0.21875, ((1, 32),), jnp.float32)
    w_up = gaussian(arg_keys[8], (D, FF), D ** -0.5, 0.21875, ((1, 32),), jnp.float32)
    w_down = gaussian(arg_keys[9], (FF, D), FF ** -0.5, 0.125, ((1, 32),), jnp.float32)
    gain_attn = jnp.clip(1.0 + 0.1 * jax.random.normal(arg_keys[10], (D,), jnp.float32), 0.5, 1.5)
    gain_ffn = jnp.clip(1.0 + 0.1 * jax.random.normal(arg_keys[11], (D,), jnp.float32), 0.5, 1.5)
    bias_table = gaussian(arg_keys[12], (BUCKETS, HEADS), 0.5, 3.0, (), jnp.float32)
    return {"inputs": inputs, "cotangent": cotangent, "lengths": lengths, "w_query": w_query, "w_key": w_key, "w_value": w_value, "w_out": w_out, "w_gate": w_gate, "w_up": w_up, "w_down": w_down, "gain_attn": gain_attn, "gain_ffn": gain_ffn, "bias_table": bias_table}


@jax.custom_vjp
def low(v):
    return lax.optimization_barrier(v.astype(jnp.bfloat16)).astype(jnp.float32)

@jax.custom_vjp
def low_back(v):
    return v

def low_keep(v):
    return (low(v), None)

def low_pass(kept, grad):
    return (grad,)

def back_keep(v):
    return (v, None)

def back_low(kept, grad):
    return (low(grad),)
low.defvjp(low_keep, low_pass)
low_back.defvjp(back_keep, back_low)
EPSILON = 1e-06
MASKED = -1000000000.0
PRECISE = lax.Precision.HIGHEST
THRESHOLDS = (12, 16, 23, 32, 46, 64, 91)

def bucket_of(offsets):
    distance = jnp.abs(offsets)
    larger = jnp.full(offsets.shape, 8, jnp.int32)
    for threshold in THRESHOLDS:
        larger = larger + (distance >= threshold).astype(jnp.int32)
    nearby = jnp.where(distance < 8, distance, larger)
    return jnp.where(offsets > 0, 16, 0).astype(jnp.int32) + nearby

def rms_factor(values):
    return lax.rsqrt(lax.optimization_barrier(jnp.mean(values * values, axis=-1, keepdims=True)) + EPSILON)

def gelu_tanh(values):
    return jax.nn.gelu(values, approximate=True)

def matmul_high(first_operand, second_operand):
    return jnp.matmul(first_operand, second_operand, precision=PRECISE)

def attend(queries, key_rows, value_rows, position_bias, lengths):
    scores = low_back(jnp.einsum('gqhd,gkhd->ghqk', queries, key_rows, precision=PRECISE))
    key_valid = jnp.arange(SLOT, dtype=jnp.int32)[None, :] < lengths[:, None]
    scores = jnp.where(key_valid[:, None, None, :], scores + position_bias[None], MASKED)
    row_max = lax.optimization_barrier(jnp.max(scores, axis=-1, keepdims=True))
    exponent = jnp.exp(scores - row_max)
    probabilities = exponent / lax.optimization_barrier(jnp.sum(exponent, axis=-1, keepdims=True))
    return jnp.einsum('ghqk,gkhd->gqhd', low(probabilities), value_rows, precision=PRECISE)

def layer_forward(params, inputs, lengths, buckets):
    w_query, w_key, w_value, w_out, w_gate, w_up, w_down, gain_attn, gain_ffn, bias_table = params
    group_size = inputs.shape[0]
    normed = low(inputs * rms_factor(inputs) * low(gain_attn))
    queries = low_back(low(matmul_high(normed, low(w_query))))
    key_rows = low_back(low(matmul_high(normed, low(w_key))))
    value_rows = low_back(low(matmul_high(normed, low(w_value))))
    position_bias = jnp.transpose(jnp.take(bias_table, buckets, axis=0), (2, 0, 1))
    head_shape = (group_size, SLOT, HEADS, HEAD_DIM)
    attended = jax.checkpoint(attend)(queries.reshape(head_shape), key_rows.reshape(head_shape), value_rows.reshape(head_shape), position_bias, lengths)
    attended = low_back(low(attended.reshape(group_size, SLOT, D)))
    hidden = inputs + low_back(matmul_high(attended, low(w_out)))
    normed_ffn = low(hidden * rms_factor(hidden) * low(gain_ffn))
    gate_value = low_back(matmul_high(normed_ffn, low(w_gate)))
    up_value = low_back(matmul_high(normed_ffn, low(w_up)))
    activated = low(gelu_tanh(gate_value) * up_value)
    return hidden + low_back(matmul_high(activated, low(w_down)))

def reference(inputs, cotangent, lengths, w_query, w_key, w_value, w_out, w_gate, w_up, w_down, gain_attn, gain_ffn, bias_table):
    params = (w_query, w_key, w_value, w_out, w_gate, w_up, w_down, gain_attn, gain_ffn, bias_table)
    offsets = jnp.arange(SLOT, dtype=jnp.int32)
    buckets = bucket_of(offsets[None, :] - offsets[:, None])
    group_count = SEQS // 2
    inputs_grouped = inputs.astype(jnp.float32).reshape(group_count, 2, SLOT, D)
    seeds_grouped = cotangent.astype(jnp.float32).reshape(group_count, 2, SLOT, D)
    lengths_grouped = lengths.reshape(group_count, 2)

    def one_group(accumulated, members):
        block_inputs, block_seeds, block_lengths = members
        valid_rows = (offsets[None, :] < block_lengths[:, None]).astype(jnp.float32)[:, :, None]

        def forward_only(weights, activations):
            return layer_forward(weights, activations, block_lengths, buckets)
        output, pullback = jax.vjp(forward_only, params, block_inputs)
        grad_params, grad_inputs = pullback(block_seeds * valid_rows)
        accumulated = jax.tree.map(jnp.add, accumulated, grad_params)
        return (accumulated, (output, grad_inputs))
    initial = jax.tree.map(jnp.zeros_like, params)
    totals, (outputs, input_grads) = lax.scan(one_group, initial, (inputs_grouped, seeds_grouped, lengths_grouped))
    return (outputs.reshape(SEQS, SLOT, D), input_grads.reshape(SEQS, SLOT, D), totals[0], totals[1], totals[2], totals[3], totals[4], totals[5], totals[6], totals[7], totals[8], totals[9])
```

```python
import functools, jax, jax.numpy as jnp
from jax import lax
from jax.experimental import pallas as pl
from jax.experimental.pallas import tpu as pltpu

HEAD_DIM = 64
LANES = 128
MASKED = -1000000000.0
VMEM_LIMIT = 60 << 20
f32, bf16 = jnp.float32, jnp.bfloat16


def dot_nt(a, b):
    return lax.dot_general(a, b, (((1,), (1,)), ((), ())), preferred_element_type=f32)


def dot_nn(a, b):
    return lax.dot_general(a, b, (((1,), (0,)), ((), ())), preferred_element_type=f32)


def dot_tn(a, b):
    return lax.dot_general(a, b, (((0,), (0,)), ((), ())), preferred_element_type=f32)


def three_pieces(x):
    hi = x.astype(bf16).astype(f32)
    mid = (x - hi).astype(bf16).astype(f32)
    return hi, mid, x - hi - mid


def skewed(row, width):
    spread = jnp.broadcast_to(row, (LANES, width))
    return pltpu.roll(spread, 0, 1, stride=1, stride_axis=0)


def lane_iota(rows):
    return lax.broadcasted_iota(jnp.int32, (rows, LANES), 1)


def key_extra(rows, length, ones_low, ones_high):
    lanes = lane_iota(rows)
    position = lax.broadcasted_iota(jnp.int32, (rows, LANES), 0)
    ones = ((lanes >= ones_low) & (lanes < ones_high)).astype(f32)
    masked = jnp.where(position < length, 0.0, MASKED)
    return jnp.where(lanes == 6, masked, ones).astype(bf16)


def forward_kernel(q_tile, k_tile, lengths, offset, q_ref, k_ref, v_ref, bias_ref, out_ref, extra_ref, keys, values, strips, scores):
    slots = k_ref.shape[1]
    tile = pl.program_id(2)
    origin = q_tile + k_tile
    chunks = slots // k_tile

    @pl.when(tile == 0)
    def _():
        keys[:, :LANES] = k_ref[0]
        keys[:, LANES:] = key_extra(slots, lengths[pl.program_id(0)], 0, 0)
        turned = v_ref[0].astype(f32).T.astype(bf16)
        for h in range(2):
            values[h, :HEAD_DIM, :] = turned[h * HEAD_DIM : (h + 1) * HEAD_DIM]
            values[h, HEAD_DIM:, :] = jnp.ones((16, slots), bf16)
            strips[h] = skewed(bias_ref[0, h : h + 1, :], strips.shape[2])

    lanes = lane_iota(q_tile)
    pair = q_ref[0].astype(f32)
    const = jnp.where(lanes == 6, 1.0, 0.0).astype(bf16)
    weights = jnp.concatenate(
        [
            jnp.concatenate([jnp.where((lanes < HEAD_DIM) == (h == 0), pair, 0.0).astype(bf16), const], axis=1)
            for h in range(2)
        ],
        axis=0,
    )
    first = offset[0] + tile * q_tile
    top = jnp.full((8, 2 * q_tile), -jnp.inf, f32)
    for c in range(chunks):
        raw = dot_nt(keys[c * k_tile : (c + 1) * k_tile, :], weights)
        base = jnp.clip(c * k_tile - first, -(k_tile + LANES), q_tile + LANES)
        for b in range(k_tile // LANES):
            at = pl.multiple_of(origin - base - b * LANES, LANES)
            both = jnp.concatenate([strips[h, :, pl.ds(at, q_tile)] for h in range(2)], axis=1)
            part = raw[b * LANES : (b + 1) * LANES] + both
            scores[c * k_tile + b * LANES : c * k_tile + (b + 1) * LANES, :] = part
            top = jnp.maximum(top, jnp.max(part.reshape(LANES // 8, 8, 2 * q_tile), axis=0))
    top = jnp.max(top, axis=0, keepdims=True)
    totals = [jnp.zeros((HEAD_DIM + 16, q_tile), f32) for h in range(2)]
    for c in range(chunks):
        weight = jnp.exp(scores[c * k_tile : (c + 1) * k_tile, :] - top).astype(bf16)
        for h in range(2):
            totals[h] += dot_nn(
                values[h, :, c * k_tile : (c + 1) * k_tile], weight[:, h * q_tile : (h + 1) * q_tile]
            )
    mixed, pieces = [], []
    for h in range(2):
        total = totals[h][HEAD_DIM : HEAD_DIM + 1]
        mixed.append(totals[h][:HEAD_DIM] / total)
        pieces += list(three_pieces(-(top[:, h * q_tile : (h + 1) * q_tile] + jnp.log(total))))
    out_ref[0] = jnp.concatenate(mixed, axis=0).T.astype(bf16)
    rows = lax.broadcasted_iota(jnp.int32, (LANES, q_tile), 0)
    stats = jnp.where(rows == 6, 1.0, 0.0)
    for n, piece in enumerate(pieces):
        stats = jnp.where(rows == n, piece, stats)
    extra_ref[0, 0] = stats.T.astype(bf16)


def strip_width(q_tile, k_tile):
    return 2 * (q_tile + k_tile) + 2 * LANES


def attention_forward(qkv, kv, lengths, offset, vector, q_tile, k_tile, pairs):
    seqs, rows, _ = qkv.shape
    keys_of, values_of, k_at, v_at = kv
    slots = keys_of.shape[1]
    width = strip_width(q_tile, k_tile)
    grid = (seqs, pairs, rows // q_tile)
    return pl.pallas_call(
        functools.partial(forward_kernel, q_tile, k_tile),
        grid_spec=pltpu.PrefetchScalarGridSpec(
            num_scalar_prefetch=2,
            grid=grid,
            in_specs=[
                pl.BlockSpec((1, q_tile, LANES), lambda s, p, i, *_: (s, i, p)),
                pl.BlockSpec((1, slots, LANES), lambda s, p, i, *_: (s, 0, p + k_at)),
                pl.BlockSpec((1, slots, LANES), lambda s, p, i, *_: (s, 0, p + v_at)),
                pl.BlockSpec((1, 2, width), lambda s, p, i, *_: (p, 0, 0)),
            ],
            out_specs=[
                pl.BlockSpec((1, q_tile, LANES), lambda s, p, i, *_: (s, i, p)),
                pl.BlockSpec((1, 1, q_tile, LANES), lambda s, p, i, *_: (s, p, i, 0)),
            ],
            scratch_shapes=[
                pltpu.VMEM((slots, 2 * LANES), bf16),
                pltpu.VMEM((2, HEAD_DIM + 16, slots), bf16),
                pltpu.VMEM((2, LANES, width), f32),
                pltpu.VMEM((slots, 2 * q_tile), f32),
            ],
        ),
        out_shape=[
            jax.ShapeDtypeStruct((seqs, rows, pairs * LANES), bf16),
            jax.ShapeDtypeStruct((seqs, pairs, rows, LANES), bf16),
        ],
        compiler_params=pltpu.CompilerParams(vmem_limit_bytes=VMEM_LIMIT),
        name="attention_forward",
    )(lengths, offset, qkv, keys_of, values_of, vector)


def backward_kernel(
    q_tile, k_tile, lengths, offset, q_ref, k_ref, v_ref, a_ref, d_ref, extra_ref, bias_ref,
    dq_ref, dk_ref, dv_ref, bias_out,
    qa, ka, va, da, q_turned, d_turned, dk_acc, dv_acc, dq_acc, strips, sums,
):
    rows, slots = q_ref.shape[1], k_ref.shape[1]
    origin = q_tile + k_tile
    width = strips.shape[2]
    chunks = slots // k_tile
    length = lengths[pl.program_id(0)]
    lanes_k, lanes_q = lane_iota(slots), lane_iota(rows)
    keys, values = k_ref[0].astype(f32), v_ref[0].astype(f32)
    for h in range(2):
        mine = (lanes_k < HEAD_DIM) == (h == 0)
        ka[h, :, :LANES] = jnp.where(mine, keys, 0.0).astype(bf16)
        ka[h, :, LANES:] = key_extra(slots, length, 3 * h, 3 * h + 3)
        va[h, :, :LANES] = jnp.where(mine, values, 0.0).astype(bf16)
        va[h, :, LANES:] = ((lanes_k >= 3 * h) & (lanes_k < 3 * h + 3)).astype(f32).astype(bf16)
        strips[h] = skewed(bias_ref[0, h : h + 1, :], width)
    qa[:, :LANES] = q_ref[0]
    qa[:, LANES:] = extra_ref[0, 0]
    grads = d_ref[0].astype(f32)
    product = grads * a_ref[0].astype(f32)
    hi = product.astype(bf16)
    low = (product - hi.astype(f32)).astype(bf16)
    row_at = lax.broadcasted_iota(jnp.int32, (LANES, LANES), 0)
    lane_at = lax.broadcasted_iota(jnp.int32, (LANES, LANES), 1)
    pick = jnp.where((lane_at < 6) & ((row_at < HEAD_DIM) == (lane_at < 3)), -1.0, 0.0).astype(bf16)
    minus_dot = dot_nn(hi, pick) + dot_nn(low, pick)
    one, two, three = three_pieces(minus_dot)
    which = lanes_q % 3
    da[:, :LANES] = d_ref[0]
    da[:, LANES:] = jnp.where(which == 0, one, jnp.where(which == 1, two, three)).astype(bf16)
    q_turned[...] = q_ref[0].astype(f32).T.astype(bf16)
    d_turned[...] = grads.T.astype(bf16)
    dk_acc[...] = jnp.zeros_like(dk_acc)
    dv_acc[...] = jnp.zeros_like(dv_acc)
    sums[...] = jnp.zeros_like(sums)

    def one_tile(i, carried):
        r0 = pl.multiple_of(i * q_tile, q_tile)
        for c in range(chunks):
            base = jnp.clip(c * k_tile - offset[0] - r0, -(k_tile + LANES), q_tile + LANES)
            cols = slice(c * k_tile, (c + 1) * k_tile)
            dq = None
            for h in range(2):
                own = slice(h * HEAD_DIM, (h + 1) * HEAD_DIM)
                raw = dot_nt(qa[pl.ds(r0, q_tile), :], ka[h, cols, :])
                back = dot_nt(da[pl.ds(r0, q_tile), :], va[h, cols, :])
                probs, grad = [], []
                for b in range(q_tile // LANES):
                    at = pl.multiple_of(origin + base - b * LANES, LANES)
                    part = slice(b * LANES, (b + 1) * LANES)
                    p = jnp.exp(raw[part] + strips[h, :, pl.ds(at, k_tile)])
                    g = p * back[part]
                    sums[h, :, pl.ds(at, k_tile)] += g
                    probs.append(p.astype(bf16))
                    grad.append(g.astype(bf16))
                probs = jnp.concatenate(probs, axis=0)
                grad = jnp.concatenate(grad, axis=0)
                dv_acc[own, cols] += dot_nn(d_turned[own, pl.ds(r0, q_tile)], probs)
                dk_acc[own, cols] += dot_nn(q_turned[own, pl.ds(r0, q_tile)], grad)
                more = dot_nn(grad, ka[h, cols, :LANES])
                dq = more if dq is None else dq + more
            if c == 0:
                dq_acc[...] = dq
            else:
                dq_acc[...] += dq
        dq_ref[0, pl.ds(r0, q_tile), :] = dq_acc[...].astype(bf16)
        return carried

    lax.fori_loop(0, rows // q_tile, one_tile, 0)
    dk_ref[0] = dk_acc[...].T.astype(bf16)
    dv_ref[0] = dv_acc[...].T.astype(bf16)
    mirror = (row_at + lane_at == LANES - 1).astype(f32)
    for h in range(2):
        flipped = lax.dot_general(
            mirror, sums[h], (((1,), (0,)), ((), ())),
            precision=lax.Precision.HIGHEST, preferred_element_type=f32,
        )
        turned = pltpu.roll(flipped, width - (LANES - 1), 1, stride=1, stride_axis=0)
        bias_out[0, 0, h : h + 1, :] = jnp.sum(turned, axis=0, keepdims=True)


def attention_backward(qkv, kv, attended, grad, extra, lengths, offset, vector, q_tile, k_tile, pairs):
    seqs, rows, _ = qkv.shape
    keys_of, values_of, k_at, v_at = kv
    slots = keys_of.shape[1]
    width = strip_width(q_tile, k_tile)
    pair_of = lambda at: lambda s, p, *_: (s, 0, p + at)
    one = pl.Buffered(2)
    spec = lambda r, at: pl.BlockSpec((1, r, LANES), pair_of(at))
    return pl.pallas_call(
        functools.partial(backward_kernel, q_tile, k_tile),
        grid_spec=pltpu.PrefetchScalarGridSpec(
            num_scalar_prefetch=2,
            grid=(seqs, pairs),
            in_specs=[
                spec(rows, 0), spec(slots, k_at), spec(slots, v_at), spec(rows, 0), spec(rows, 0),
                pl.BlockSpec((1, 1, rows, LANES), lambda s, p, *_: (s, p, 0, 0)),
                pl.BlockSpec((1, 2, width), lambda s, p, *_: (p, 0, 0)),
            ],
            out_specs=[
                spec(rows, 0), spec(slots, 0), spec(slots, 0),
                pl.BlockSpec((1, 1, 2, width), lambda s, p, *_: (s, p, 0, 0)),
            ],
            scratch_shapes=[
                pltpu.VMEM((rows, 2 * LANES), bf16),
                pltpu.VMEM((2, slots, 2 * LANES), bf16),
                pltpu.VMEM((2, slots, 2 * LANES), bf16),
                pltpu.VMEM((rows, 2 * LANES), bf16),
                pltpu.VMEM((LANES, rows), bf16),
                pltpu.VMEM((LANES, rows), bf16),
                pltpu.VMEM((LANES, slots), f32),
                pltpu.VMEM((LANES, slots), f32),
                pltpu.VMEM((q_tile, LANES), f32),
                pltpu.VMEM((2, LANES, width), f32),
                pltpu.VMEM((2, LANES, width), f32),
            ],
        ),
        out_shape=[
            jax.ShapeDtypeStruct((seqs, rows, pairs * LANES), bf16),
            jax.ShapeDtypeStruct((seqs, slots, pairs * LANES), bf16),
            jax.ShapeDtypeStruct((seqs, slots, pairs * LANES), bf16),
            jax.ShapeDtypeStruct((seqs, pairs, 2, width), f32),
        ],
        compiler_params=pltpu.CompilerParams(vmem_limit_bytes=VMEM_LIMIT),
        name="attention_backward",
    )(lengths, offset, qkv, keys_of, values_of, attended, grad, extra, vector)


THRESHOLDS = (12, 16, 23, 32, 46, 64, 91)


def bucket_of(offsets):
    distance = jnp.abs(offsets)
    larger = jnp.full(offsets.shape, 8, jnp.int32)
    for threshold in THRESHOLDS:
        larger = larger + (distance >= threshold).astype(jnp.int32)
    nearby = jnp.where(distance < 8, distance, larger)
    return jnp.where(offsets > 0, 16, 0).astype(jnp.int32) + nearby


def bias_onehot(q_tile, k_tile, flip):
    width = strip_width(q_tile, k_tile)
    lane = jnp.arange(width, dtype=jnp.int32)
    lane = jnp.where(lane >= width - LANES, lane - width, lane)
    offs = lane - (q_tile + k_tile)
    if flip:
        offs = -offs
    return (bucket_of(offs)[:, None] == jnp.arange(32, dtype=jnp.int32)[None, :]).astype(f32)


from jax.sharding import PartitionSpec as P

D = 768
HEADS = 12
PAIRS = HEADS // 2
FF = 2048
BUCKETS = 32
EPSILON = 1e-06
PRECISE = lax.Precision.HIGHEST
BOTH = ("dp", "fsdp")
FF_CHUNK = 512


def rms_factor(values):
    return lax.rsqrt(jnp.mean(values * values, axis=-1, keepdims=True) + EPSILON)


def norm_back(grad_normed, values, factor, gain):
    scaled = grad_normed * gain
    return factor * scaled - values * (factor * factor * factor) * jnp.mean(
        scaled * values, axis=-1, keepdims=True
    )


def project_kernel(x_ref, w_ref, gain_ref, out_ref):
    x = x_ref[...].astype(f32)
    normed = (x * rms_factor(x) * gain_ref[...]).astype(bf16)
    for n in range(3):
        part = slice(n * D, (n + 1) * D)
        out_ref[:, part] = dot_nt(normed, w_ref[:, part]).astype(bf16)


def project(x, weights, gain, tile):
    tokens = x.shape[0]
    return pl.pallas_call(
        project_kernel,
        grid=(tokens // tile,),
        in_specs=[
            pl.BlockSpec((tile, D), lambda i: (i, 0)),
            pl.BlockSpec((D, 3 * D), lambda i: (0, 0)),
            pl.BlockSpec((1, D), lambda i: (0, 0)),
        ],
        out_specs=pl.BlockSpec((tile, 3 * D), lambda i: (i, 0)),
        out_shape=jax.ShapeDtypeStruct((tokens, 3 * D), bf16),
        compiler_params=pltpu.CompilerParams(vmem_limit_bytes=VMEM_LIMIT),
        name="project",
    )(x, weights, gain)


def ffn_kernel(
    tile, rows, away, lengths, place, x_ref, a_ref, c_ref, wod_ref, wgu_ref, gain_ref,
    own_ref, away_ref, gh_ref, ga_ref, dod_out, dgu_out, gain_out,
    dod, dgu, gain_acc, hidden_ref, nf_ref, seed_ref, out_acc, dnf_acc, sems,
):
    step = pl.program_id(0)
    steps = pl.num_programs(0)
    at = tile_at(step, place, away, steps)

    @pl.when(step == 0)
    def _():
        dod[...] = jnp.zeros_like(dod)
        dgu[...] = jnp.zeros_like(dgu)
        gain_acc[...] = jnp.zeros_like(gain_acc)

    per_seq = rows // tile
    seq = at // per_seq
    first = place[1] + (at - seq * per_seq) * tile
    position = first + lax.broadcasted_iota(jnp.int32, (tile, D), 0)
    hidden_ref[...] = x_ref[...].astype(f32) + dot_nt(a_ref[...], wod_ref[:, :D])
    hidden = hidden_ref[...]
    factor = rms_factor(hidden)
    gain = gain_ref[...]
    nf_ref[...] = (hidden * factor * gain).astype(bf16)
    seed_ref[...] = jnp.where(position < lengths[seq], c_ref[...].astype(f32), 0.0).astype(bf16)
    out_acc[...] = hidden
    dnf_acc[...] = jnp.zeros_like(dnf_acc)

    def chunk(c, carried):
        f0 = pl.multiple_of(c * FF_CHUNK, FF_CHUNK)
        ff = pl.ds(f0, FF_CHUNK)
        down = pl.ds(pl.multiple_of(D + f0, LANES), FF_CHUNK)
        nf, seed = nf_ref[...], seed_ref[...]
        gate = dot_nt(nf, wgu_ref[ff, :D])
        up = dot_nt(nf, wgu_ref[ff, D:])
        back = dot_nn(seed, wod_ref[:, down])
        square = gate * gate
        root = 0.7978845608028654
        tanh = jnp.tanh(gate * (root + (root * 0.044715) * square))
        half = 0.5 + 0.5 * tanh
        active = gate * half
        slope = half + (0.5 * gate) * (1.0 - tanh * tanh) * (root + (3.0 * root * 0.044715) * square)
        activated = (active * up).astype(bf16)
        grad_gate = (back * up * slope).astype(bf16)
        grad_up = (back * active).astype(bf16)
        out_acc[...] += dot_nt(activated, wod_ref[:, down])
        dnf_acc[...] += dot_nn(grad_gate, wgu_ref[ff, :D]) + dot_nn(grad_up, wgu_ref[ff, D:])
        dod[:, down] += dot_tn(seed, activated)
        dgu[ff, :D] += dot_tn(grad_gate, nf)
        dgu[ff, D:] += dot_tn(grad_up, nf)
        return carried

    lax.fori_loop(0, FF // FF_CHUNK, chunk, 0)
    hidden = hidden_ref[...]
    factor = rms_factor(hidden)
    dnf = dnf_acc[...]
    gain_acc[...] += jnp.sum(dnf * hidden * factor, axis=0, keepdims=True)
    grad_hidden = seed_ref[...].astype(f32) + norm_back(dnf, hidden, factor, gain)
    gh_ref[...] = grad_hidden
    branch = grad_hidden.astype(bf16)
    ga_ref[...] = dot_nn(branch, wod_ref[:, :D]).astype(bf16)
    dod[:, :D] += dot_tn(branch, a_ref[...])

    @pl.when(step < away)
    def _():
        away_ref[...] = out_acc[...].astype(bf16)

    @pl.when(step >= away)
    def _():
        own_ref[...] = out_acc[...]

    @pl.when(step == steps - 1)
    def _():
        gain_out[...] = gain_acc[...]
        one = pltpu.make_async_copy(dod, dod_out, sems.at[0])
        two = pltpu.make_async_copy(dgu, dgu_out, sems.at[1])
        one.start()
        two.start()
        one.wait()
        two.wait()


def tile_at(step, place, away, steps):
    if away == 0:
        return step
    return (step + away * (1 - place[0])) % steps


def away_index(away):
    return lambda i, *_: (jnp.minimum(i, max(away, 1) - 1), 0)


def own_index(away):
    return lambda i, *_: (jnp.maximum(i - away, 0), 0)


def ffn(x, attended, cotangent, wod, wgu, gain, lengths, place, tile, rows, away):
    tokens = x.shape[0]
    steps = tokens // tile
    by_tile = lambda i, lengths, place: (tile_at(i, place, away, steps), 0)
    whole = lambda i, *_: (0, 0)
    single = pl.Buffered(1)
    return pl.pallas_call(
        functools.partial(ffn_kernel, tile, rows, away),
        grid_spec=pltpu.PrefetchScalarGridSpec(
            num_scalar_prefetch=2,
            grid=(steps,),
            in_specs=[
                pl.BlockSpec((tile, D), by_tile),
                pl.BlockSpec((tile, D), by_tile),
                pl.BlockSpec((tile, D), by_tile),
                pl.BlockSpec((D, D + FF), whole, pipeline_mode=single),
                pl.BlockSpec((FF, 2 * D), whole, pipeline_mode=single),
                pl.BlockSpec((1, D), whole),
            ],
            out_specs=[
                pl.BlockSpec((tile, D), own_index(away)),
                pl.BlockSpec((tile, D), away_index(away)),
                pl.BlockSpec((tile, D), by_tile),
                pl.BlockSpec((tile, D), by_tile),
                pl.BlockSpec(memory_space=pl.ANY),
                pl.BlockSpec(memory_space=pl.ANY),
                pl.BlockSpec((1, D), whole),
            ],
            scratch_shapes=[
                pltpu.VMEM((D, D + FF), f32),
                pltpu.VMEM((FF, 2 * D), f32),
                pltpu.VMEM((1, D), f32),
                pltpu.VMEM((tile, D), f32),
                pltpu.VMEM((tile, D), bf16),
                pltpu.VMEM((tile, D), bf16),
                pltpu.VMEM((tile, D), f32),
                pltpu.VMEM((tile, D), f32),
                pltpu.SemaphoreType.DMA((2,)),
            ],
        ),
        out_shape=[
            jax.ShapeDtypeStruct((tokens - away * tile, D), f32),
            jax.ShapeDtypeStruct((max(away, 1) * tile, D), bf16),
            jax.ShapeDtypeStruct((tokens, D), f32),
            jax.ShapeDtypeStruct((tokens, D), bf16),
            jax.ShapeDtypeStruct((D, D + FF), f32),
            jax.ShapeDtypeStruct((FF, 2 * D), f32),
            jax.ShapeDtypeStruct((1, D), f32),
        ],
        compiler_params=pltpu.CompilerParams(vmem_limit_bytes=VMEM_LIMIT),
        name="ffn",
    )(lengths, place, x, attended, cotangent, wod, wgu, gain)


def finish_kernel(
    away, place, x_ref, dq_ref, dk_ref, dv_ref, gh_ref, w_ref, gain_ref, gain_two_ref,
    own_ref, away_ref, dw_ref, acc,
):
    step = pl.program_id(0)

    @pl.when(step == 0)
    def _():
        dw_ref[...] = jnp.zeros_like(dw_ref)
        acc[...] = jnp.zeros_like(acc)

    x = x_ref[...].astype(f32)
    factor = rms_factor(x)
    gain = gain_ref[...]
    normed = (x * factor * gain).astype(bf16)
    grad_normed = None
    for n, ref in enumerate((dq_ref, dk_ref, dv_ref)):
        part = slice(n * D, (n + 1) * D)
        grad = ref[...]
        dw_ref[:, part] += dot_tn(grad, normed)
        more = dot_nn(grad, w_ref[:, part])
        grad_normed = more if grad_normed is None else grad_normed + more
    acc[...] += jnp.sum(grad_normed * x * factor, axis=0, keepdims=True)
    grad_x = gh_ref[...] + norm_back(grad_normed, x, factor, gain)

    @pl.when(step < away)
    def _():
        away_ref[...] = grad_x.astype(bf16)

    @pl.when(step >= away)
    def _():
        own_ref[...] = grad_x

    @pl.when(step == pl.num_programs(0) - 1)
    def _():
        rows = lax.broadcasted_iota(jnp.int32, (LANES, D), 0)
        both = jnp.where(rows == 0, acc[...], jnp.where(rows == 1, gain_two_ref[...], 0.0))
        dw_ref[:, 3 * D :] = both.T


def finish(x, dq, dk, dv, gh, weights, gain, gain_two_grad, place, tile, away):
    tokens = x.shape[0]
    steps = tokens // tile
    by_tile = lambda i, place: (tile_at(i, place, away, steps), 0)
    whole = lambda i, *_: (0, 0)
    block = pl.BlockSpec((tile, D), by_tile)
    return pl.pallas_call(
        functools.partial(finish_kernel, away),
        grid_spec=pltpu.PrefetchScalarGridSpec(
            num_scalar_prefetch=1,
            grid=(steps,),
            in_specs=[
                block, block, block, block, block,
                pl.BlockSpec((D, 3 * D), whole),
                pl.BlockSpec((1, D), whole),
                pl.BlockSpec((1, D), whole),
            ],
            out_specs=[
                pl.BlockSpec((tile, D), own_index(away)),
                pl.BlockSpec((tile, D), away_index(away)),
                pl.BlockSpec((D, 3 * D + LANES), whole),
            ],
            scratch_shapes=[pltpu.VMEM((1, D), f32)],
        ),
        out_shape=[
            jax.ShapeDtypeStruct((tokens - away * tile, D), f32),
            jax.ShapeDtypeStruct((max(away, 1) * tile, D), bf16),
            jax.ShapeDtypeStruct((D, 3 * D + LANES), f32),
        ],
        compiler_params=pltpu.CompilerParams(vmem_limit_bytes=VMEM_LIMIT),
        name="finish",
    )(place, x, dq, dk, dv, gh, weights, gain, gain_two_grad)


def swap_in(block, side):
    mine = lax.dynamic_index_in_dim(block, side, 0, keepdims=False)
    other = lax.dynamic_index_in_dim(block, 1 - side, 0, keepdims=False)
    come = lax.ppermute(other, "fsdp", [(0, 1), (1, 0)])
    return jnp.where(side == 0, jnp.concatenate([mine, come]), jnp.concatenate([come, mine]))


def swap_out(own, away, side):
    come = lax.ppermute(away, "fsdp", [(0, 1), (1, 0)]).astype(f32)
    return jnp.where(side == 0, jnp.stack([own, come]), jnp.stack([come, own]))


def turned(weight):
    return weight.astype(bf16).T


def per_device(
    sides, inputs, cotangent, lengths, w_query, w_key, w_value, w_out, w_gate, w_up, w_down,
    gain_attn, gain_ffn, bias_table,
):
    seqs, own_rows, _ = inputs.shape
    slots = own_rows * sides
    side = lax.axis_index("fsdp")
    share = gain_attn.shape[0]
    gains = jnp.pad(jnp.stack([gain_attn, gain_ffn], axis=1).astype(bf16), ((0, 0), (0, LANES - 2)))
    packed = jnp.concatenate([turned(w_query), turned(w_key), turned(w_value), gains], axis=1)
    wqkv = lax.all_gather(packed, BOTH, axis=0, tiled=True)
    gain_rows = wqkv[:, 3 * D : 3 * D + 2].astype(f32).T
    wod = lax.all_gather(jnp.concatenate([turned(w_out), turned(w_down)], axis=1), BOTH, axis=0, tiled=True)
    wgu = lax.all_gather(jnp.concatenate([turned(w_gate), turned(w_up)], axis=1), BOTH, axis=0, tiled=True)
    swap = seqs == 2 and sides == 2
    if swap:
        x, seed = swap_in(inputs, side), swap_in(cotangent, side)
        lengths = lax.dynamic_slice_in_dim(lengths, side, 1)
        seqs, rows, first = 1, slots, jnp.zeros((), jnp.int32)
    else:
        x, seed = inputs.reshape(-1, D), cotangent.reshape(-1, D)
        rows, first = own_rows, side * own_rows
    tile = min(512, own_rows)
    away = own_rows // tile if swap else 0
    place = jnp.stack([side, first]).astype(jnp.int32)
    origin = place[1:]
    one_hot = bias_onehot(tile, 512, False)
    vector = jnp.dot(one_hot, bias_table, precision=PRECISE).T.reshape(PAIRS, 2, -1)
    flipped = jnp.dot(bias_onehot(tile, 512, True), bias_table, precision=PRECISE).T.reshape(PAIRS, 2, -1)

    qkv = project(x, wqkv, gain_rows[0:1], tile).reshape(seqs, rows, 3 * D)
    if rows < slots:
        kv = lax.all_gather(qkv[:, :, D:], "fsdp", axis=1, tiled=True)
        sources = (kv, kv, 0, PAIRS)
    else:
        sources = (qkv, qkv, PAIRS, 2 * PAIRS)
    attended, extra = attention_forward(qkv, sources, lengths, origin, flipped, tile, 512, PAIRS)
    own, away_out, grad_hidden, grad_attended, dod, dgu, gain_two = ffn(
        x, attended.reshape(-1, D), seed, wod, wgu, gain_rows[1:2], lengths, place, tile, rows, away
    )
    if swap:
        output = swap_out(own, away_out, side)
    else:
        output = own.reshape(seqs, rows, D)
    out_down = lax.psum_scatter(dod.astype(bf16), BOTH, scatter_dimension=0, tiled=True).astype(f32)
    gate_up = lax.psum_scatter(dgu.astype(bf16), BOTH, scatter_dimension=0, tiled=True).astype(f32)
    dq, dk, dv, strips = attention_backward(
        qkv, sources, attended, grad_attended.reshape(seqs, rows, D), extra, lengths, origin, vector,
        tile, 512, PAIRS,
    )
    if rows < slots:
        dk = lax.psum_scatter(dk, "fsdp", scatter_dimension=1, tiled=True)
        dv = lax.psum_scatter(dv, "fsdp", scatter_dimension=1, tiled=True)
    diagonals = jnp.sum(strips, axis=0).reshape(HEADS, -1)
    table = lax.psum(jnp.dot(diagonals, one_hot, precision=PRECISE).T, BOTH)
    flat = lambda a: a.reshape(-1, D)
    own, away_grad, dw = finish(
        x, flat(dq), flat(dk), flat(dv), grad_hidden, wqkv, gain_rows[0:1], gain_two, place, tile, away
    )
    if swap:
        grad_inputs = swap_out(own, away_grad, side)
    else:
        grad_inputs = own.reshape(seqs, rows, D)
    query_key = lax.psum_scatter(dw.astype(bf16), BOTH, scatter_dimension=0, tiled=True).astype(f32)
    return (
        output,
        grad_inputs,
        query_key[:, :D].T,
        query_key[:, D : 2 * D].T,
        query_key[:, 2 * D : 3 * D].T,
        out_down[:, :D].T,
        gate_up[:, :D].T,
        gate_up[:, D:].T,
        out_down[:, D:].T,
        query_key[:, 3 * D],
        query_key[:, 3 * D + 1],
        table,
    )


def solution(mesh):
    tokens = P("dp", "fsdp", None)
    columns = P(None, BOTH)
    return jax.shard_map(
        functools.partial(per_device, mesh.shape["fsdp"]),
        mesh=mesh,
        in_specs=(tokens, tokens, P("dp")) + (columns,) * 7 + (P(BOTH), P(BOTH), P()),
        out_specs=(tokens, tokens) + (columns,) * 7 + (P(BOTH), P(BOTH), P()),
        check_vma=False,
    )
```

```python
import functools, jax, jax.numpy as jnp
from jax import lax
from jax.experimental import pallas as pl
from jax.experimental.pallas import tpu as pltpu

HEAD_DIM = 64
LANES = 128
SUB_TILE = 256
MASKED = -1000000000.0
VMEM_LIMIT = 60 << 20


def cost(microseconds):
    return pl.CostEstimate(flops=int(1.1e9 * microseconds), bytes_accessed=1 << 20, transcendentals=0)
f32, bf16 = jnp.float32, jnp.bfloat16


def dot_nt(a, b):
    return lax.dot_general(a, b, (((1,), (1,)), ((), ())), preferred_element_type=f32)


def dot_nn(a, b):
    return lax.dot_general(a, b, (((1,), (0,)), ((), ())), preferred_element_type=f32)


def dot_tn(a, b):
    return lax.dot_general(a, b, (((0,), (0,)), ((), ())), preferred_element_type=f32)


def three_pieces(x):
    hi = x.astype(bf16).astype(f32)
    mid = (x - hi).astype(bf16).astype(f32)
    return hi, mid, x - hi - mid


def skewed(row, width):
    spread = jnp.broadcast_to(row, (LANES, width))
    return pltpu.roll(spread, 0, 1, stride=1, stride_axis=0)


def lane_iota(rows):
    return lax.broadcasted_iota(jnp.int32, (rows, LANES), 1)


def key_extra(rows, length, ones_low, ones_high):
    lanes = lane_iota(rows)
    position = lax.broadcasted_iota(jnp.int32, (rows, LANES), 0)
    ones = ((lanes >= ones_low) & (lanes < ones_high)).astype(f32)
    masked = jnp.where(position < length, 0.0, MASKED)
    return jnp.where(lanes == 6, masked, ones).astype(bf16)


def forward_kernel(q_tile, k_tile, lengths, offset, q_ref, k_ref, v_ref, bias_ref, out_ref, extra_ref, keys, values, strips, scores_even, scores_odd):
    slots = k_ref.shape[1]
    tile = pl.program_id(2)
    origin = q_tile + k_tile
    chunks = slots // k_tile

    @pl.when(tile == 0)
    def _():
        keys[:, :LANES] = k_ref[0]
        keys[:, LANES:] = key_extra(slots, lengths[pl.program_id(0)], 0, 0)
        turned = v_ref[0].astype(f32).T.astype(bf16)
        for h in range(2):
            values[h, :HEAD_DIM, :] = turned[h * HEAD_DIM : (h + 1) * HEAD_DIM]
            values[h, HEAD_DIM:, :] = jnp.ones((16, slots), bf16)
            strips[h] = skewed(bias_ref[0, h : h + 1, :], strips.shape[2])

    lanes = lane_iota(q_tile)
    pair = q_ref[0].astype(f32)
    const = jnp.where(lanes == 6, 1.0, 0.0).astype(bf16)
    weights = [
        jnp.concatenate([jnp.where((lanes < HEAD_DIM) == (h == 0), pair, 0.0).astype(bf16), const], axis=1)
        for h in range(2)
    ]
    first = offset[0] + tile * q_tile
    sub = min(SUB_TILE, q_tile)
    chains = [(u, h) for u in range(q_tile // sub) for h in range(2)]
    scores = (scores_even, scores_odd)
    tops, totals = {}, {}
    for n in range(len(chains) + 1):
        top = jnp.full((8, sub), -jnp.inf, f32)
        total = jnp.zeros((HEAD_DIM + 16, sub), f32)
        for c in range(chunks):
            rows = slice(c * k_tile, (c + 1) * k_tile)
            if n < len(chains):
                u, h = chains[n]
                raw = dot_nt(keys[rows, :], weights[h][u * sub : (u + 1) * sub])
                base = jnp.clip(c * k_tile - first - u * sub, -(k_tile + LANES), q_tile + LANES)
                for b in range(k_tile // LANES):
                    at = pl.multiple_of(origin - base - b * LANES, LANES)
                    part = raw[b * LANES : (b + 1) * LANES] + strips[h, :, pl.ds(at, sub)]
                    scores[n % 2][c * k_tile + b * LANES : c * k_tile + (b + 1) * LANES, :] = part
                    top = jnp.maximum(top, jnp.max(part.reshape(LANES // 8, 8, sub), axis=0))
            if n > 0:
                weight = jnp.exp(scores[(n - 1) % 2][rows, :] - tops[n - 1]).astype(bf16)
                total += dot_nn(values[chains[n - 1][1], :, rows], weight)
        tops[n] = jnp.max(top, axis=0, keepdims=True)
        totals[n - 1] = total
    top = [jnp.concatenate([tops[n] for n in range(h, len(chains), 2)], axis=1) for h in range(2)]
    totals = [jnp.concatenate([totals[n] for n in range(h, len(chains), 2)], axis=1) for h in range(2)]
    mixed, pieces = [], []
    for h in range(2):
        total = totals[h][HEAD_DIM : HEAD_DIM + 1]
        mixed.append(totals[h][:HEAD_DIM] / total)
        pieces += list(three_pieces(-(top[h] + jnp.log(total))))
    out_ref[0] = jnp.concatenate(mixed, axis=0).T.astype(bf16)
    rows = lax.broadcasted_iota(jnp.int32, (LANES, q_tile), 0)
    stats = jnp.where(rows == 6, 1.0, 0.0)
    for n, piece in enumerate(pieces):
        stats = jnp.where(rows == n, piece, stats)
    extra_ref[0, 0] = stats.T.astype(bf16)


def strip_width(q_tile, k_tile):
    return 2 * (q_tile + k_tile) + 2 * LANES


def attention_forward(qkv, kv, lengths, offset, vector, q_tile, k_tile, pairs):
    seqs, rows, _ = qkv.shape
    keys_of, values_of, k_at, v_at = kv
    slots = keys_of.shape[1]
    width = strip_width(q_tile, k_tile)
    grid = (seqs, pairs, rows // q_tile)
    return pl.pallas_call(
        functools.partial(forward_kernel, q_tile, k_tile),
        grid_spec=pltpu.PrefetchScalarGridSpec(
            num_scalar_prefetch=2,
            grid=grid,
            in_specs=[
                pl.BlockSpec((1, q_tile, LANES), lambda s, p, i, *_: (s, i, p)),
                pl.BlockSpec((1, slots, LANES), lambda s, p, i, *_: (s, 0, p + k_at)),
                pl.BlockSpec((1, slots, LANES), lambda s, p, i, *_: (s, 0, p + v_at)),
                pl.BlockSpec((1, 2, width), lambda s, p, i, *_: (p, 0, 0)),
            ],
            out_specs=[
                pl.BlockSpec((1, q_tile, LANES), lambda s, p, i, *_: (s, i, p)),
                pl.BlockSpec((1, 1, q_tile, LANES), lambda s, p, i, *_: (s, p, i, 0)),
            ],
            scratch_shapes=[
                pltpu.VMEM((slots, 2 * LANES), bf16),
                pltpu.VMEM((2, HEAD_DIM + 16, slots), bf16),
                pltpu.VMEM((2, LANES, width), f32),
                pltpu.VMEM((slots, min(SUB_TILE, q_tile)), f32),
                pltpu.VMEM((slots, min(SUB_TILE, q_tile)), f32),
            ],
        ),
        out_shape=[
            jax.ShapeDtypeStruct((seqs, rows, pairs * LANES), bf16),
            jax.ShapeDtypeStruct((seqs, pairs, rows, LANES), bf16),
        ],
        compiler_params=pltpu.CompilerParams(vmem_limit_bytes=VMEM_LIMIT),
        cost_estimate=cost(100),
        name="attention_forward",
    )(lengths, offset, qkv, keys_of, values_of, vector)


def backward_kernel(
    q_tile, k_tile, lengths, offset, q_ref, k_ref, v_ref, a_ref, d_ref, extra_ref, bias_ref,
    dq_ref, dk_ref, dv_ref, bias_out,
    qa, ka, va, da, q_turned, d_turned, dk_acc, dv_acc, dq_acc, strips, sums,
):
    rows, slots = q_ref.shape[1], k_ref.shape[1]
    origin = q_tile + k_tile
    width = strips.shape[2]
    chunks = slots // k_tile
    length = lengths[pl.program_id(0)]
    lanes_k, lanes_q = lane_iota(slots), lane_iota(rows)
    keys, values = k_ref[0].astype(f32), v_ref[0].astype(f32)
    for h in range(2):
        mine = (lanes_k < HEAD_DIM) == (h == 0)
        ka[h, :, :LANES] = jnp.where(mine, keys, 0.0).astype(bf16)
        ka[h, :, LANES:] = key_extra(slots, length, 3 * h, 3 * h + 3)
        va[h, :, :LANES] = jnp.where(mine, values, 0.0).astype(bf16)
        va[h, :, LANES:] = ((lanes_k >= 3 * h) & (lanes_k < 3 * h + 3)).astype(f32).astype(bf16)
        strips[h] = skewed(bias_ref[0, h : h + 1, :], width)
    qa[:, :LANES] = q_ref[0]
    qa[:, LANES:] = extra_ref[0, 0]
    grads = d_ref[0].astype(f32)
    product = grads * a_ref[0].astype(f32)
    hi = product.astype(bf16)
    low = (product - hi.astype(f32)).astype(bf16)
    row_at = lax.broadcasted_iota(jnp.int32, (LANES, LANES), 0)
    lane_at = lax.broadcasted_iota(jnp.int32, (LANES, LANES), 1)
    pick = jnp.where((lane_at < 6) & ((row_at < HEAD_DIM) == (lane_at < 3)), -1.0, 0.0).astype(bf16)
    minus_dot = dot_nn(hi, pick) + dot_nn(low, pick)
    one, two, three = three_pieces(minus_dot)
    which = lanes_q % 3
    da[:, :LANES] = d_ref[0]
    da[:, LANES:] = jnp.where(which == 0, one, jnp.where(which == 1, two, three)).astype(bf16)
    q_turned[...] = q_ref[0].astype(f32).T.astype(bf16)
    d_turned[...] = grads.T.astype(bf16)
    dk_acc[...] = jnp.zeros_like(dk_acc)
    dv_acc[...] = jnp.zeros_like(dv_acc)
    sums[...] = jnp.zeros_like(sums)

    def one_tile(i, carried):
        r0 = pl.multiple_of(i * q_tile, q_tile)
        units = [(c, h) for c in range(chunks) for h in range(2)]

        def products(c, h):
            cols = slice(c * k_tile, (c + 1) * k_tile)
            raw = dot_nt(qa[pl.ds(r0, q_tile), :], ka[h, cols, :])
            back = dot_nt(da[pl.ds(r0, q_tile), :], va[h, cols, :])
            return raw, back

        ahead = products(*units[0])
        for n, (c, h) in enumerate(units):
            raw, back = ahead
            if n + 1 < len(units):
                ahead = products(*units[n + 1])
            base = jnp.clip(c * k_tile - offset[0] - r0, -(k_tile + LANES), q_tile + LANES)
            cols = slice(c * k_tile, (c + 1) * k_tile)
            own = slice(h * HEAD_DIM, (h + 1) * HEAD_DIM)
            probs, grad = [], []
            for b in range(q_tile // LANES):
                at = pl.multiple_of(origin + base - b * LANES, LANES)
                part = slice(b * LANES, (b + 1) * LANES)
                p = jnp.exp(raw[part] + strips[h, :, pl.ds(at, k_tile)])
                g = p * back[part]
                sums[h, :, pl.ds(at, k_tile)] += g
                probs.append(p.astype(bf16))
                grad.append(g.astype(bf16))
            probs = jnp.concatenate(probs, axis=0)
            grad = jnp.concatenate(grad, axis=0)
            dv_acc[own, cols] += dot_nn(d_turned[own, pl.ds(r0, q_tile)], probs)
            dk_acc[own, cols] += dot_nn(q_turned[own, pl.ds(r0, q_tile)], grad)
            dq = dot_nn(grad, ka[h, cols, :LANES])
            if n == 0:
                dq_acc[...] = dq
            else:
                dq_acc[...] += dq
        dq_ref[0, pl.ds(r0, q_tile), :] = dq_acc[...].astype(bf16)
        return carried

    lax.fori_loop(0, rows // q_tile, one_tile, 0)
    dk_ref[0] = dk_acc[...].T.astype(bf16)
    dv_ref[0] = dv_acc[...].T.astype(bf16)
    mirror = (row_at + lane_at == LANES - 1).astype(f32)
    for h in range(2):
        flipped = lax.dot_general(
            mirror, sums[h], (((1,), (0,)), ((), ())),
            precision=lax.Precision.HIGHEST, preferred_element_type=f32,
        )
        turned = pltpu.roll(flipped, width - (LANES - 1), 1, stride=1, stride_axis=0)
        bias_out[0, 0, h : h + 1, :] = jnp.sum(turned, axis=0, keepdims=True)


def attention_backward(qkv, kv, attended, grad, extra, lengths, offset, vector, q_tile, k_tile, low, pairs):
    seqs, rows, _ = qkv.shape
    keys_of, values_of, k_at, v_at = kv
    slots = keys_of.shape[1]
    width = strip_width(q_tile, k_tile)
    pair_of = lambda at: lambda s, p, *_: (s, 0, p + at)
    spec = lambda r, at: pl.BlockSpec((1, r, LANES), pair_of(at))
    return pl.pallas_call(
        functools.partial(backward_kernel, q_tile, k_tile),
        grid_spec=pltpu.PrefetchScalarGridSpec(
            num_scalar_prefetch=2,
            grid=(seqs, pairs),
            in_specs=[
                spec(rows, low), spec(slots, k_at + low), spec(slots, v_at + low), spec(rows, low), spec(rows, low),
                pl.BlockSpec((1, 1, rows, LANES), lambda s, p, *_: (s, p + low, 0, 0)),
                pl.BlockSpec((1, 2, width), lambda s, p, *_: (p + low, 0, 0)),
            ],
            out_specs=[
                spec(rows, 0), spec(slots, 0), spec(slots, 0),
                pl.BlockSpec((1, 1, 2, width), lambda s, p, *_: (s, p, 0, 0)),
            ],
            scratch_shapes=[
                pltpu.VMEM((rows, 2 * LANES), bf16),
                pltpu.VMEM((2, slots, 2 * LANES), bf16),
                pltpu.VMEM((2, slots, 2 * LANES), bf16),
                pltpu.VMEM((rows, 2 * LANES), bf16),
                pltpu.VMEM((LANES, rows), bf16),
                pltpu.VMEM((LANES, rows), bf16),
                pltpu.VMEM((LANES, slots), f32),
                pltpu.VMEM((LANES, slots), f32),
                pltpu.VMEM((q_tile, LANES), f32),
                pltpu.VMEM((2, LANES, width), f32),
                pltpu.VMEM((2, LANES, width), f32),
            ],
        ),
        out_shape=[
            jax.ShapeDtypeStruct((seqs, rows, pairs * LANES), bf16),
            jax.ShapeDtypeStruct((seqs, slots, pairs * LANES), bf16),
            jax.ShapeDtypeStruct((seqs, slots, pairs * LANES), bf16),
            jax.ShapeDtypeStruct((seqs, pairs, 2, width), f32),
        ],
        compiler_params=pltpu.CompilerParams(vmem_limit_bytes=VMEM_LIMIT),
        cost_estimate=cost(30 * pairs),
        name="attention_backward",
    )(lengths, offset, qkv, keys_of, values_of, attended, grad, extra, vector)


THRESHOLDS = (12, 16, 23, 32, 46, 64, 91)


def bucket_of(offsets):
    distance = jnp.abs(offsets)
    larger = jnp.full(offsets.shape, 8, jnp.int32)
    for threshold in THRESHOLDS:
        larger = larger + (distance >= threshold).astype(jnp.int32)
    nearby = jnp.where(distance < 8, distance, larger)
    return jnp.where(offsets > 0, 16, 0).astype(jnp.int32) + nearby


def bias_onehot(q_tile, k_tile, flip):
    width = strip_width(q_tile, k_tile)
    lane = jnp.arange(width, dtype=jnp.int32)
    lane = jnp.where(lane >= width - LANES, lane - width, lane)
    offs = lane - (q_tile + k_tile)
    if flip:
        offs = -offs
    return (bucket_of(offs)[:, None] == jnp.arange(32, dtype=jnp.int32)[None, :]).astype(f32)


from jax.sharding import PartitionSpec as P

D = 768
HEADS = 12
PAIRS = HEADS // 2
FF = 2048
BUCKETS = 32
EPSILON = 1e-06
PRECISE = lax.Precision.HIGHEST
BOTH = ("dp", "fsdp")
FF_CHUNK = 512
WO = slice(FF_CHUNK, FF_CHUNK + D)
GROUP = 2
FORWARD_TILES = (1024, 512)
BACKWARD_TILES = (512, 256)


def rms_factor(values):
    return lax.rsqrt(jnp.mean(values * values, axis=-1, keepdims=True) + EPSILON)


def norm_back(grad_normed, values, factor, gain):
    scaled = grad_normed * gain
    return factor * scaled - values * (factor * factor * factor) * jnp.mean(
        scaled * values, axis=-1, keepdims=True
    )


def project_kernel(x_ref, w_ref, gain_ref, out_ref):
    x = x_ref[...].astype(f32)
    normed = (x * rms_factor(x) * gain_ref[...]).astype(bf16)
    for n in range(3):
        part = slice(n * D, (n + 1) * D)
        out_ref[:, part] = dot_nt(normed, w_ref[:, part]).astype(bf16)


def project(x, weights, gain, tile):
    tokens = x.shape[0]
    return pl.pallas_call(
        project_kernel,
        grid=(tokens // tile,),
        in_specs=[
            pl.BlockSpec((tile, D), lambda i: (i, 0)),
            pl.BlockSpec((D, 3 * D), lambda i: (0, 0)),
            pl.BlockSpec((1, D), lambda i: (0, 0)),
        ],
        out_specs=pl.BlockSpec((tile, 3 * D), lambda i: (i, 0)),
        out_shape=jax.ShapeDtypeStruct((tokens, 3 * D), bf16),
        compiler_params=pltpu.CompilerParams(vmem_limit_bytes=VMEM_LIMIT),
        cost_estimate=cost(12),
        name="project",
    )(x, weights, gain)


def ffn_kernel(
    tile, rows, away, lengths, place, x_ref, a_ref, c_ref, one_ref, two_ref, wgu_ref, gain_ref,
    own_ref, away_ref, gh_ref, ga_ref, dod_out, dgu_out, gain_out,
    dod, dgu, gain_acc, hidden_ref, nf_ref, seed_ref, out_acc, dnf_acc, sems,
):
    step = pl.program_id(0)
    steps = pl.num_programs(0)
    at = tile_at(step, place, away, steps)

    @pl.when(step == 0)
    def _():
        dod[...] = jnp.zeros_like(dod)
        dgu[...] = jnp.zeros_like(dgu)
        gain_acc[...] = jnp.zeros_like(gain_acc)

    per_seq = rows // tile
    seq = at // per_seq
    first = place[1] + (at - seq * per_seq) * tile
    position = first + lax.broadcasted_iota(jnp.int32, (tile, D), 0)
    hidden_ref[...] = x_ref[...].astype(f32) + dot_nt(a_ref[...], two_ref[:, WO])
    hidden = hidden_ref[...]
    factor = rms_factor(hidden)
    gain = gain_ref[...]
    nf_ref[...] = (hidden * factor * gain).astype(bf16)
    seed_ref[...] = jnp.where(position < lengths[seq], c_ref[...].astype(f32), 0.0).astype(bf16)
    out_acc[...] = hidden
    dnf_acc[...] = jnp.zeros_like(dnf_acc)

    for f0 in range(0, FF, FF_CHUNK):
        ff = slice(f0, f0 + FF_CHUNK)
        down = slice(D + f0, D + f0 + FF_CHUNK)
        w_down = one_ref[:, ff] if f0 < 2 * D else two_ref[:, :FF_CHUNK]
        nf, seed = nf_ref[...], seed_ref[...]
        gate = dot_nt(nf, wgu_ref[ff, :D])
        up = dot_nt(nf, wgu_ref[ff, D:])
        back = dot_nn(seed, w_down)
        square = gate * gate
        root = 0.7978845608028654
        tanh = jnp.tanh(gate * (root + (root * 0.044715) * square))
        half = 0.5 + 0.5 * tanh
        active = gate * half
        slope = half + (0.5 * gate) * (1.0 - tanh * tanh) * (root + (3.0 * root * 0.044715) * square)
        activated = (active * up).astype(bf16)
        grad_gate = (back * up * slope).astype(bf16)
        grad_up = (back * active).astype(bf16)
        out_acc[...] += dot_nt(activated, w_down)
        dnf_acc[...] += dot_nn(grad_gate, wgu_ref[ff, :D]) + dot_nn(grad_up, wgu_ref[ff, D:])
        dod[:, down] += dot_tn(seed, activated)
        dgu[ff, :D] += dot_tn(grad_gate, nf)
        dgu[ff, D:] += dot_tn(grad_up, nf)
    hidden = hidden_ref[...]
    factor = rms_factor(hidden)
    dnf = dnf_acc[...]
    gain_acc[...] += jnp.sum(dnf * hidden * factor, axis=0, keepdims=True)
    grad_hidden = seed_ref[...].astype(f32) + norm_back(dnf, hidden, factor, gain)
    gh_ref[...] = grad_hidden
    branch = grad_hidden.astype(bf16)
    ga_ref[...] = dot_nn(branch, two_ref[:, WO]).astype(bf16)
    dod[:, :D] += dot_tn(branch, a_ref[...])

    @pl.when(step < away)
    def _():
        away_ref[...] = out_acc[...].astype(bf16)

    @pl.when(step >= away)
    def _():
        own_ref[...] = out_acc[...]

    @pl.when(step == steps - 1)
    def _():
        gain_out[...] = gain_acc[...]
        one = pltpu.make_async_copy(dod, dod_out, sems.at[0])
        two = pltpu.make_async_copy(dgu, dgu_out, sems.at[1])
        one.start()
        two.start()
        one.wait()
        two.wait()


def tile_at(step, place, away, steps):
    if away == 0:
        return step
    return (step + away * (1 - place[0])) % steps


def away_index(away):
    return lambda i, *_: (jnp.minimum(i, max(away, 1) - 1), 0)


def own_index(away):
    return lambda i, *_: (jnp.maximum(i - away, 0), 0)


def ffn(x, attended, cotangent, w_one, w_two, wgu, gain, lengths, place, tile, rows, away):
    tokens = x.shape[0]
    steps = tokens // tile
    by_tile = lambda i, lengths, place: (tile_at(i, place, away, steps), 0)
    whole = lambda i, *_: (0, 0)
    single = pl.Buffered(1)
    return pl.pallas_call(
        functools.partial(ffn_kernel, tile, rows, away),
        grid_spec=pltpu.PrefetchScalarGridSpec(
            num_scalar_prefetch=2,
            grid=(steps,),
            in_specs=[
                pl.BlockSpec((tile, D), by_tile),
                pl.BlockSpec((tile, D), by_tile),
                pl.BlockSpec((tile, D), by_tile),
                pl.BlockSpec((D, 2 * D), whole, pipeline_mode=single),
                pl.BlockSpec((D, 2 * D), whole, pipeline_mode=single),
                pl.BlockSpec((FF, 2 * D), whole, pipeline_mode=single),
                pl.BlockSpec((1, D), whole),
            ],
            out_specs=[
                pl.BlockSpec((tile, D), own_index(away)),
                pl.BlockSpec((tile, D), away_index(away)),
                pl.BlockSpec((tile, D), by_tile),
                pl.BlockSpec((tile, D), by_tile),
                pl.BlockSpec(memory_space=pl.ANY),
                pl.BlockSpec(memory_space=pl.ANY),
                pl.BlockSpec((1, D), whole),
            ],
            scratch_shapes=[
                pltpu.VMEM((D, D + FF), f32),
                pltpu.VMEM((FF, 2 * D), f32),
                pltpu.VMEM((1, D), f32),
                pltpu.VMEM((tile, D), f32),
                pltpu.VMEM((tile, D), bf16),
                pltpu.VMEM((tile, D), bf16),
                pltpu.VMEM((tile, D), f32),
                pltpu.VMEM((tile, D), f32),
                pltpu.SemaphoreType.DMA((2,)),
            ],
        ),
        out_shape=[
            jax.ShapeDtypeStruct((tokens - away * tile, D), f32),
            jax.ShapeDtypeStruct((max(away, 1) * tile, D), bf16),
            jax.ShapeDtypeStruct((tokens, D), f32),
            jax.ShapeDtypeStruct((tokens, D), bf16),
            jax.ShapeDtypeStruct((D, D + FF), f32),
            jax.ShapeDtypeStruct((FF, 2 * D), f32),
            jax.ShapeDtypeStruct((1, D), f32),
        ],
        compiler_params=pltpu.CompilerParams(vmem_limit_bytes=VMEM_LIMIT),
        cost_estimate=cost(95),
        name="ffn",
    )(lengths, place, x, attended, cotangent, w_one, w_two, wgu, gain)


def weights_kernel(pieces, x_ref, gain_ref, *refs):
    grads, dw_ref = refs[:-1], refs[-1]

    @pl.when(pl.program_id(0) == 0)
    def _():
        dw_ref[...] = jnp.zeros_like(dw_ref)

    x = x_ref[...].astype(f32)
    normed = (x * rms_factor(x) * gain_ref[...]).astype(bf16)
    for n in range(3):
        row = 0
        for ref in grads[n * pieces : (n + 1) * pieces]:
            rows = slice(row, row + ref.shape[1])
            dw_ref[rows, n * D : (n + 1) * D] += dot_tn(ref[...], normed)
            row += ref.shape[1]


def finish_weights(x, gain, dq, dk, dv, tile):
    tokens = x.shape[0]
    grads = [*dq, *dk, *dv]
    return pl.pallas_call(
        functools.partial(weights_kernel, len(dq)),
        grid=(tokens // tile,),
        in_specs=[pl.BlockSpec((tile, D), lambda i: (i, 0)), pl.BlockSpec((1, D), lambda i: (0, 0))]
        + [pl.BlockSpec((tile, g.shape[1]), lambda i: (i, 0)) for g in grads],
        out_specs=pl.BlockSpec((sum(g.shape[1] for g in dq), 3 * D), lambda i: (0, 0)),
        out_shape=jax.ShapeDtypeStruct((sum(g.shape[1] for g in dq), 3 * D), f32),
        compiler_params=pltpu.CompilerParams(vmem_limit_bytes=VMEM_LIMIT),
        cost_estimate=cost(14),
        name="finish_weights",
    )(x, gain, *grads)


def finish_kernel(away, pieces, place, x_ref, gh_ref, w_ref, gain_ref, *refs):
    grads, (own_ref, away_ref, gain_out) = refs[:-3], refs[-3:]
    step = pl.program_id(0)

    @pl.when(step == 0)
    def _():
        gain_out[...] = jnp.zeros_like(gain_out)

    grad_normed = None
    for n in range(3):
        row = 0
        for ref in grads[n * pieces : (n + 1) * pieces]:
            more = dot_nn(ref[...], w_ref[row : row + ref.shape[1], n * D : (n + 1) * D])
            grad_normed = more if grad_normed is None else grad_normed + more
            row += ref.shape[1]
    x = x_ref[...].astype(f32)
    factor = rms_factor(x)
    gain_out[...] += jnp.sum(grad_normed * x * factor, axis=0, keepdims=True)
    grad_x = gh_ref[...] + norm_back(grad_normed, x, factor, gain_ref[...])

    @pl.when(step < away)
    def _():
        away_ref[...] = grad_x.astype(bf16)

    @pl.when(step >= away)
    def _():
        own_ref[...] = grad_x


def finish_inputs(x, gh, weights, gain, dq, dk, dv, place, tile, away):
    tokens = x.shape[0]
    steps = tokens // tile
    by_tile = lambda i, place: (tile_at(i, place, away, steps), 0)
    whole = lambda i, *_: (0, 0)
    grads = [*dq, *dk, *dv]
    return pl.pallas_call(
        functools.partial(finish_kernel, away, len(dq)),
        grid_spec=pltpu.PrefetchScalarGridSpec(
            num_scalar_prefetch=1,
            grid=(steps,),
            in_specs=[
                pl.BlockSpec((tile, D), by_tile),
                pl.BlockSpec((tile, D), by_tile),
                pl.BlockSpec((D, 3 * D), whole),
                pl.BlockSpec((1, D), whole),
            ]
            + [pl.BlockSpec((tile, g.shape[1]), by_tile) for g in grads],
            out_specs=[
                pl.BlockSpec((tile, D), own_index(away)),
                pl.BlockSpec((tile, D), away_index(away)),
                pl.BlockSpec((1, D), whole),
            ],
        ),
        out_shape=[
            jax.ShapeDtypeStruct((tokens - away * tile, D), f32),
            jax.ShapeDtypeStruct((max(away, 1) * tile, D), bf16),
            jax.ShapeDtypeStruct((1, D), f32),
        ],
        compiler_params=pltpu.CompilerParams(vmem_limit_bytes=VMEM_LIMIT),
        cost_estimate=cost(16),
        name="finish_inputs",
    )(place, x, gh, weights, gain, *grads)


Y, CORE, X, Z = 1, 2, 4, 8
SQUARE_DEVICES = 32


def from_peer(value, flip):
    return lax.ppermute(value, BOTH, [(n, n ^ flip) for n in range(SQUARE_DEVICES)])


def bit(me, which):
    return (me // which) % 2


def gather_rows(shard, *alongside):
    me = lax.axis_index(BOTH)
    n, lanes = shard.shape
    z = me // Z
    parts = [shard] + [from_peer(shard, k * Z) for k in (1, 2, 3)]
    parts = after(parts, *alongside[0:1])
    column = jnp.stack([pick(parts, z ^ at) for at in range(4)])
    square = [column] + [from_peer(column, k) for k in (Y, X, X + Y)]
    square = after(square, *alongside[1:2])
    corner = bit(me, X) * 2 + bit(me, Y)
    plane = jnp.stack([pick(square, corner ^ at) for at in range(4)], axis=1).reshape(4, 2, 2, n, lanes)
    other = after(from_peer(plane, CORE), *alongside[2:3])
    core = bit(me, CORE)
    both = jnp.stack([jnp.where(core == 0, plane, other), jnp.where(core == 0, other, plane)], axis=2)
    return both.reshape(32 * n, lanes)


def pick(parts, at):
    out = parts[0]
    for n in range(1, len(parts)):
        out = jnp.where(at == n, parts[n], out)
    return out


def scatter_rows(total):
    me = lax.axis_index(BOTH)
    n, lanes = total.shape[0] // 32, total.shape[1]
    blocks = total.reshape(4, 2, 2, 2, n, lanes)
    core, x, y, z = bit(me, CORE), bit(me, X), bit(me, Y), me // Z
    take = lambda a, at, axis: lax.dynamic_index_in_dim(a, at, axis, keepdims=False)
    sent = from_peer(take(blocks, 1 - core, 2).astype(bf16), CORE)
    sent = yield sent
    mine = (take(blocks, core, 2) + sent.astype(f32)).reshape(4, 4, n, lanes)
    corner = 2 * x + y
    sent = [from_peer(take(mine, corner ^ k, 1).astype(bf16), (k // 2) * X + (k % 2) * Y) for k in (1, 2, 3)]
    sent = yield sent
    mine = take(mine, corner, 1) + (sent[0].astype(f32) + sent[1].astype(f32) + sent[2].astype(f32))
    sent = [from_peer(take(mine, z ^ k, 0).astype(bf16), k * Z) for k in (1, 2, 3)]
    sent = yield sent
    yield take(mine, z, 0) + (sent[0].astype(f32) + sent[1].astype(f32) + sent[2].astype(f32))


def scatter_plain(total):
    sent = yield total.astype(bf16)
    sent = yield sent
    sent = yield sent
    yield lax.psum_scatter(sent, BOTH, scatter_dimension=0, tiled=True).astype(f32)


def sum_all(value):
    value = value + from_peer(value, CORE)
    value = value + (from_peer(value, Y) + from_peer(value, X) + from_peer(value, X + Y))
    return value + (from_peer(value, Z) + from_peer(value, 2 * Z) + from_peer(value, 3 * Z))


def swap_start(block, side):
    other = lax.dynamic_index_in_dim(block, 1 - side, 0, keepdims=False)
    return lax.ppermute(other, "fsdp", [(0, 1), (1, 0)])


def swap_in(block, come, side):
    mine = lax.dynamic_index_in_dim(block, side, 0, keepdims=False)
    return jnp.where(side == 0, jnp.concatenate([mine, come]), jnp.concatenate([come, mine]))


def swap_out(own, come, side):
    come = come.astype(f32)
    return jnp.where(side == 0, jnp.stack([own, come]), jnp.stack([come, own]))


def turned(weight):
    return weight.astype(bf16).T


def after(value, *others):
    if not others:
        return value
    return lax.optimization_barrier((value, *others))[0]


def per_device(
    sizes, inputs, cotangent, lengths, w_query, w_key, w_value, w_out, w_gate, w_up, w_down,
    gain_attn, gain_ffn, bias_table,
):
    seqs, own_rows, _ = inputs.shape
    sides = sizes["fsdp"]
    slots = own_rows * sides
    side = lax.axis_index("fsdp")
    swap = seqs == 2 and sides == 2
    if sizes["dp"] * sides == SQUARE_DEVICES and sides == 2:
        gather, scatter, total = gather_rows, scatter_rows, sum_all
    else:
        gather = lambda a, *b: lax.all_gather(a, BOTH, axis=0, tiled=True)
        scatter = scatter_plain
        total = lambda a: lax.psum(a, BOTH)
    if swap:
        other = lax.dynamic_index_in_dim(inputs, 1 - side, 0, keepdims=False)
        other, w_query, w_key, w_value = lax.optimization_barrier((other, w_query, w_key, w_value))
        come = [lax.ppermute(part, "fsdp", [(0, 1), (1, 0)]) for part in jnp.split(other, (384, 768))]
    else:
        come = []
    gains = jnp.pad(jnp.stack([gain_attn, gain_ffn], axis=1).astype(bf16), ((0, 0), (0, LANES - 2)))
    packed = jnp.concatenate([turned(w_query), turned(w_key), turned(w_value), gains], axis=1)
    w_out, w_gate, w_up, w_down, packed = lax.optimization_barrier((w_out, w_gate, w_up, w_down, packed))
    wqkv = gather(packed, *come)
    gain_rows = wqkv[:, 3 * D : 3 * D + 2].astype(f32).T
    rest = jnp.concatenate(
        [
            turned(w_down)[:, : 2 * D],
            jnp.pad(jnp.concatenate([turned(w_down)[:, 2 * D :], turned(w_out)], axis=1), ((0, 0), (0, 256))),
            jnp.concatenate([turned(w_gate), turned(w_up)], axis=1),
        ]
    )
    rest = lax.all_gather(after(rest, wqkv), BOTH)
    share, ff_share = gain_attn.shape[0], w_gate.shape[1]
    w_one = rest[:, :share].reshape(D, 2 * D)
    w_two = rest[:, share : 2 * share].reshape(D, 2 * D)
    wgu = rest[:, 2 * share :].reshape(FF, 2 * D)
    if swap:
        x = swap_in(inputs, jnp.concatenate(come), side)
        lengths = lax.dynamic_slice_in_dim(lengths, side, 1)
        seqs, rows, first = 1, slots, jnp.zeros((), jnp.int32)
    else:
        x = inputs.reshape(-1, D)
        rows, first = own_rows, side * own_rows
    tile = min(512, own_rows)
    away = own_rows // tile if swap else 0
    place = jnp.stack([side, first]).astype(jnp.int32)
    origin = place[1:]
    ahead_tiles = (min(FORWARD_TILES[0], rows), FORWARD_TILES[1])
    back_tiles = (min(BACKWARD_TILES[0], rows), BACKWARD_TILES[1])
    one_hot = bias_onehot(*back_tiles, False)
    vector = jnp.dot(one_hot, bias_table, precision=PRECISE).T.reshape(PAIRS, 2, -1)
    flipped = jnp.dot(bias_onehot(*ahead_tiles, True), bias_table, precision=PRECISE).T.reshape(PAIRS, 2, -1)

    qkv = project(x, wqkv, gain_rows[0:1], tile).reshape(seqs, rows, 3 * D)
    if swap:
        cotangent = after(cotangent, x)
        seed_come = swap_start(cotangent, side)
    if rows < slots:
        kv = lax.all_gather(qkv[:, :, D:], "fsdp", axis=1, tiled=True)
        sources = (kv, kv, 0, PAIRS)
    else:
        sources = (qkv, qkv, PAIRS, 2 * PAIRS)
    attended, extra = attention_forward(qkv, sources, lengths, origin, flipped, *ahead_tiles, PAIRS)
    if swap:
        seed = swap_in(cotangent, after(seed_come, attended), side)
    else:
        seed = cotangent.reshape(-1, D)
    own, away_out, grad_hidden, grad_attended, dod, dgu, gain_two = ffn(
        x, attended.reshape(-1, D), seed, w_one, w_two, wgu, gain_rows[1:2], lengths, place, tile, rows, away
    )
    grad_attended = grad_attended.reshape(seqs, rows, D)
    dq, dk, dv, strips = [], [], [], []
    scatters = [scatter(dod), scatter(dgu)]
    moving = [next(s) for s in scatters]
    back = []
    if swap:
        back = [lax.ppermute(away_out, "fsdp", [(0, 1), (1, 0)])]
    for low in range(0, PAIRS, GROUP):
        one, two, three, strip = attention_backward(
            qkv, sources, attended, grad_attended, extra, lengths, origin, vector, *back_tiles, low, GROUP
        )
        if rows < slots:
            two = lax.psum_scatter(two, "fsdp", scatter_dimension=1, tiled=True)
            three = lax.psum_scatter(three, "fsdp", scatter_dimension=1, tiled=True)
        dq.append(one.reshape(-1, GROUP * LANES))
        dk.append(two.reshape(-1, GROUP * LANES))
        dv.append(three.reshape(-1, GROUP * LANES))
        strips.append(strip)
        moving, back, extra, dq, dk, dv = lax.optimization_barrier((moving, back, extra, dq, dk, dv))
        moving = [s.send(m) for s, m in zip(scatters, moving)]
    out_down, gate_up = moving
    if swap:
        output = swap_out(own, back[0], side)
    else:
        output = own.reshape(seqs, rows, D)
    dq = after(dq, output)
    dw = finish_weights(x, gain_rows[0:1], dq, dk, dv, tile)
    scatter_qk = scatter(dw)
    moving = next(scatter_qk)
    own, away_grad, gain_one = finish_inputs(
        x, grad_hidden, wqkv, gain_rows[0:1], after(dq, dw), dk, dv, place, tile, away
    )
    moving, own, gain_one = lax.optimization_barrier((moving, own, gain_one))
    if swap:
        back = [lax.ppermute(part, "fsdp", [(0, 1), (1, 0)]) for part in jnp.split(away_grad, 2)]
    else:
        back = [own, own]
    moving = scatter_qk.send(moving)
    diagonals = jnp.sum(jnp.concatenate(strips, axis=1), axis=0).reshape(HEADS, -1)
    table = jnp.dot(diagonals, one_hot, precision=PRECISE).T
    small = jnp.concatenate([gain_one, gain_two, jnp.pad(table.reshape(1, -1), ((0, 0), (0, D - BUCKETS * HEADS)))])
    small = total(small)
    moving, back[0], small = lax.optimization_barrier((moving, back[0], small))
    moving = scatter_qk.send(moving)
    moving, back[1] = lax.optimization_barrier((moving, back[1]))
    query_key = scatter_qk.send(moving)
    gain_shares = lax.dynamic_slice_in_dim(small[:2], lax.axis_index(BOTH) * gain_attn.shape[0], gain_attn.shape[0], 1)
    if swap:
        grad_inputs = swap_out(own, jnp.concatenate(back), side)
    else:
        grad_inputs = own.reshape(seqs, rows, D)
    return (
        output,
        grad_inputs,
        query_key[:, :D].T,
        query_key[:, D : 2 * D].T,
        query_key[:, 2 * D : 3 * D].T,
        out_down[:, :D].T,
        gate_up[:, :D].T,
        gate_up[:, D:].T,
        out_down[:, D:].T,
        gain_shares[0],
        gain_shares[1],
        small[2, : BUCKETS * HEADS].reshape(BUCKETS, HEADS),
    )


def solution(mesh):
    tokens = P("dp", "fsdp", None)
    columns = P(None, BOTH)
    return jax.shard_map(
        functools.partial(per_device, dict(mesh.shape)),
        mesh=mesh,
        in_specs=(tokens, tokens, P("dp")) + (columns,) * 7 + (P(BOTH), P(BOTH), P()),
        out_specs=(tokens, tokens) + (columns,) * 7 + (P(BOTH), P(BOTH), P()),
        check_vma=False,
    )
```

```python
import functools, jax, jax.numpy as jnp
from jax import lax
from jax.experimental import pallas as pl
from jax.experimental.pallas import tpu as pltpu

HEAD_DIM = 64
LANES = 128
SUB_TILE = 256
MASKED = -1000000000.0
VMEM_LIMIT = 60 << 20


def cost(microseconds):
    return pl.CostEstimate(flops=int(1.1e9 * microseconds), bytes_accessed=1 << 20, transcendentals=0)
f32, bf16 = jnp.float32, jnp.bfloat16


def dot_nt(a, b):
    return lax.dot_general(a, b, (((1,), (1,)), ((), ())), preferred_element_type=f32)


def dot_nn(a, b):
    return lax.dot_general(a, b, (((1,), (0,)), ((), ())), preferred_element_type=f32)


def dot_tn(a, b):
    return lax.dot_general(a, b, (((0,), (0,)), ((), ())), preferred_element_type=f32)


def three_pieces(x):
    hi = x.astype(bf16).astype(f32)
    mid = (x - hi).astype(bf16).astype(f32)
    return hi, mid, x - hi - mid


def skewed(row, width):
    spread = jnp.broadcast_to(row, (LANES, width))
    return pltpu.roll(spread, 0, 1, stride=1, stride_axis=0)


def lane_iota(rows):
    return lax.broadcasted_iota(jnp.int32, (rows, LANES), 1)


def key_extra(rows, length, ones_low, ones_high):
    lanes = lane_iota(rows)
    position = lax.broadcasted_iota(jnp.int32, (rows, LANES), 0)
    ones = ((lanes >= ones_low) & (lanes < ones_high)).astype(f32)
    masked = jnp.where(position < length, 0.0, MASKED)
    return jnp.where(lanes == 6, masked, ones).astype(bf16)


def forward_kernel(q_tile, k_tile, lengths, offset, q_ref, k_ref, v_ref, bias_ref, out_ref, extra_ref, keys, values, strips, scores_even, scores_odd):
    slots = k_ref.shape[1]
    tile = pl.program_id(2)
    origin = q_tile + k_tile
    chunks = slots // k_tile

    @pl.when(tile == 0)
    def _():
        keys[:, :LANES] = k_ref[0]
        keys[:, LANES:] = key_extra(slots, lengths[pl.program_id(0)], 0, 0)
        turned = v_ref[0].astype(f32).T.astype(bf16)
        for h in range(2):
            values[h, :HEAD_DIM, :] = turned[h * HEAD_DIM : (h + 1) * HEAD_DIM]
            values[h, HEAD_DIM:, :] = jnp.ones((16, slots), bf16)
            strips[h] = skewed(bias_ref[0, h : h + 1, :], strips.shape[2])

    lanes = lane_iota(q_tile)
    pair = q_ref[0].astype(f32)
    const = jnp.where(lanes == 6, 1.0, 0.0).astype(bf16)
    weights = [
        jnp.concatenate([jnp.where((lanes < HEAD_DIM) == (h == 0), pair, 0.0).astype(bf16), const], axis=1)
        for h in range(2)
    ]
    first = offset[0] + tile * q_tile
    sub = min(SUB_TILE, q_tile)
    chains = [(u, h) for u in range(q_tile // sub) for h in range(2)]
    scores = (scores_even, scores_odd)
    tops, totals = {}, {}
    for n in range(len(chains) + 1):
        top = jnp.full((8, sub), -jnp.inf, f32)
        total = jnp.zeros((HEAD_DIM + 16, sub), f32)
        for c in range(chunks):
            rows = slice(c * k_tile, (c + 1) * k_tile)
            if n < len(chains):
                u, h = chains[n]
                raw = dot_nt(keys[rows, :], weights[h][u * sub : (u + 1) * sub])
                base = jnp.clip(c * k_tile - first - u * sub, -(k_tile + LANES), q_tile + LANES)
                for b in range(k_tile // LANES):
                    at = pl.multiple_of(origin - base - b * LANES, LANES)
                    part = raw[b * LANES : (b + 1) * LANES] + strips[h, :, pl.ds(at, sub)]
                    scores[n % 2][c * k_tile + b * LANES : c * k_tile + (b + 1) * LANES, :] = part
                    top = jnp.maximum(top, jnp.max(part.reshape(LANES // 8, 8, sub), axis=0))
            if n > 0:
                weight = jnp.exp(scores[(n - 1) % 2][rows, :] - tops[n - 1]).astype(bf16)
                total += dot_nn(values[chains[n - 1][1], :, rows], weight)
        tops[n] = jnp.max(top, axis=0, keepdims=True)
        totals[n - 1] = total
    top = [jnp.concatenate([tops[n] for n in range(h, len(chains), 2)], axis=1) for h in range(2)]
    totals = [jnp.concatenate([totals[n] for n in range(h, len(chains), 2)], axis=1) for h in range(2)]
    mixed, pieces = [], []
    for h in range(2):
        total = totals[h][HEAD_DIM : HEAD_DIM + 1]
        mixed.append(totals[h][:HEAD_DIM] / total)
        pieces += list(three_pieces(-(top[h] + jnp.log(total))))
    out_ref[0] = jnp.concatenate(mixed, axis=0).T.astype(bf16)
    rows = lax.broadcasted_iota(jnp.int32, (LANES, q_tile), 0)
    stats = jnp.where(rows == 6, 1.0, 0.0)
    for n, piece in enumerate(pieces):
        stats = jnp.where(rows == n, piece, stats)
    extra_ref[0, 0] = stats.T.astype(bf16)


def strip_width(q_tile, k_tile):
    return 2 * (q_tile + k_tile) + 2 * LANES


def attention_forward(qkv, kv, lengths, offset, vector, q_tile, k_tile, pairs):
    seqs, rows, _ = qkv.shape
    keys_of, values_of, k_at, v_at = kv
    slots = keys_of.shape[1]
    width = strip_width(q_tile, k_tile)
    grid = (seqs, pairs, rows // q_tile)
    return pl.pallas_call(
        functools.partial(forward_kernel, q_tile, k_tile),
        grid_spec=pltpu.PrefetchScalarGridSpec(
            num_scalar_prefetch=2,
            grid=grid,
            in_specs=[
                pl.BlockSpec((1, q_tile, LANES), lambda s, p, i, *_: (s, i, p)),
                pl.BlockSpec((1, slots, LANES), lambda s, p, i, *_: (s, 0, p + k_at)),
                pl.BlockSpec((1, slots, LANES), lambda s, p, i, *_: (s, 0, p + v_at)),
                pl.BlockSpec((1, 2, width), lambda s, p, i, *_: (p, 0, 0)),
            ],
            out_specs=[
                pl.BlockSpec((1, q_tile, LANES), lambda s, p, i, *_: (s, i, p)),
                pl.BlockSpec((1, 1, q_tile, LANES), lambda s, p, i, *_: (s, p, i, 0)),
            ],
            scratch_shapes=[
                pltpu.VMEM((slots, 2 * LANES), bf16),
                pltpu.VMEM((2, HEAD_DIM + 16, slots), bf16),
                pltpu.VMEM((2, LANES, width), f32),
                pltpu.VMEM((slots, min(SUB_TILE, q_tile)), f32),
                pltpu.VMEM((slots, min(SUB_TILE, q_tile)), f32),
            ],
        ),
        out_shape=[
            jax.ShapeDtypeStruct((seqs, rows, pairs * LANES), bf16),
            jax.ShapeDtypeStruct((seqs, pairs, rows, LANES), bf16),
        ],
        compiler_params=pltpu.CompilerParams(vmem_limit_bytes=VMEM_LIMIT),
        cost_estimate=cost(100),
        name="attention_forward",
    )(lengths, offset, qkv, keys_of, values_of, vector)


def backward_kernel(
    q_tile, k_tile, lengths, offset, q_ref, k_ref, v_ref, a_ref, d_ref, extra_ref, bias_ref,
    dq_ref, dk_ref, dv_ref, bias_out,
    qa, ka, va, da, q_turned, d_turned, dk_acc, dv_acc, dq_acc, strips, sums,
):
    rows, slots = q_ref.shape[1], k_ref.shape[1]
    origin = q_tile + k_tile
    width = strips.shape[2]
    chunks = slots // k_tile
    length = lengths[pl.program_id(0)]
    lanes_k, lanes_q = lane_iota(slots), lane_iota(rows)
    half = lax.broadcasted_iota(jnp.int32, (1, LANES), 1) < HEAD_DIM
    for h in range(2):
        mine = (half == (h == 0)).astype(f32).astype(bf16)
        ka[h, :, :LANES] = k_ref[0] * mine
        ka[h, :, LANES:] = key_extra(slots, length, 3 * h, 3 * h + 3)
        va[h, :, :LANES] = v_ref[0] * mine
        va[h, :, LANES:] = ((lanes_k >= 3 * h) & (lanes_k < 3 * h + 3)).astype(f32).astype(bf16)
        strips[h] = skewed(bias_ref[0, h : h + 1, :], width)
    qa[:, :LANES] = q_ref[0]
    qa[:, LANES:] = extra_ref[0, 0]
    grads = d_ref[0].astype(f32)
    product = grads * a_ref[0].astype(f32)
    hi = product.astype(bf16)
    low = (product - hi.astype(f32)).astype(bf16)
    row_at = lax.broadcasted_iota(jnp.int32, (LANES, LANES), 0)
    lane_at = lax.broadcasted_iota(jnp.int32, (LANES, LANES), 1)
    pick = jnp.where((lane_at < 6) & ((row_at < HEAD_DIM) == (lane_at < 3)), -1.0, 0.0).astype(bf16)
    minus_dot = dot_nn(hi, pick) + dot_nn(low, pick)
    one, two, three = three_pieces(minus_dot)
    which = lanes_q % 3
    da[:, :LANES] = d_ref[0]
    da[:, LANES:] = jnp.where(which == 0, one, jnp.where(which == 1, two, three)).astype(bf16)
    q_turned[...] = q_ref[0].T
    d_turned[...] = d_ref[0].T
    dk_acc[...] = jnp.zeros_like(dk_acc)
    dv_acc[...] = jnp.zeros_like(dv_acc)
    sums[...] = jnp.zeros_like(sums)

    def one_tile(i, carried):
        r0 = pl.multiple_of(i * q_tile, q_tile)
        units = [(c, h) for c in range(chunks) for h in range(2)]

        def products(c, h):
            cols = slice(c * k_tile, (c + 1) * k_tile)
            raw = dot_nt(qa[pl.ds(r0, q_tile), :], ka[h, cols, :])
            back = dot_nt(da[pl.ds(r0, q_tile), :], va[h, cols, :])
            return raw, back

        ahead = products(*units[0])
        for n, (c, h) in enumerate(units):
            raw, back = ahead
            if n + 1 < len(units):
                ahead = products(*units[n + 1])
            base = jnp.clip(c * k_tile - offset[0] - r0, -(k_tile + LANES), q_tile + LANES)
            cols = slice(c * k_tile, (c + 1) * k_tile)
            own = slice(h * HEAD_DIM, (h + 1) * HEAD_DIM)
            probs, grad = [], []
            for b in range(q_tile // LANES):
                at = pl.multiple_of(origin + base - b * LANES, LANES)
                part = slice(b * LANES, (b + 1) * LANES)
                p = jnp.exp(raw[part] + strips[h, :, pl.ds(at, k_tile)])
                g = p * back[part]
                sums[h, :, pl.ds(at, k_tile)] += g
                probs.append(p.astype(bf16))
                grad.append(g.astype(bf16))
            probs = jnp.concatenate(probs, axis=0)
            grad = jnp.concatenate(grad, axis=0)
            dv_acc[own, cols] += dot_nn(d_turned[own, pl.ds(r0, q_tile)], probs)
            dk_acc[own, cols] += dot_nn(q_turned[own, pl.ds(r0, q_tile)], grad)
            dq = dot_nn(grad, ka[h, cols, :LANES])
            if n == 0:
                dq_acc[...] = dq
            else:
                dq_acc[...] += dq
        dq_ref[0, pl.ds(r0, q_tile), :] = dq_acc[...].astype(bf16)
        return carried

    lax.fori_loop(0, rows // q_tile, one_tile, 0)
    dk_ref[0] = dk_acc[...].T.astype(bf16)
    dv_ref[0] = dv_acc[...].T.astype(bf16)
    mirror = (row_at + lane_at == LANES - 1).astype(f32)
    for h in range(2):
        flipped = lax.dot_general(
            mirror, sums[h], (((1,), (0,)), ((), ())),
            precision=lax.Precision.HIGHEST, preferred_element_type=f32,
        )
        turned = pltpu.roll(flipped, width - (LANES - 1), 1, stride=1, stride_axis=0)
        bias_out[0, 0, h : h + 1, :] = jnp.sum(turned, axis=0, keepdims=True)


def attention_backward(qkv, kv, attended, grad, extra, lengths, offset, vector, q_tile, k_tile, low, pairs):
    seqs, rows, _ = qkv.shape
    keys_of, values_of, k_at, v_at = kv
    slots = keys_of.shape[1]
    width = strip_width(q_tile, k_tile)
    pair_of = lambda at: lambda s, p, *_: (s, 0, p + at)
    spec = lambda r, at: pl.BlockSpec((1, r, LANES), pair_of(at))
    return pl.pallas_call(
        functools.partial(backward_kernel, q_tile, k_tile),
        grid_spec=pltpu.PrefetchScalarGridSpec(
            num_scalar_prefetch=2,
            grid=(seqs, pairs),
            in_specs=[
                spec(rows, low), spec(slots, k_at + low), spec(slots, v_at + low), spec(rows, low), spec(rows, low),
                pl.BlockSpec((1, 1, rows, LANES), lambda s, p, *_: (s, p + low, 0, 0)),
                pl.BlockSpec((1, 2, width), lambda s, p, *_: (p + low, 0, 0)),
            ],
            out_specs=[
                spec(rows, 0), spec(slots, 0), spec(slots, 0),
                pl.BlockSpec((1, 1, 2, width), lambda s, p, *_: (s, p, 0, 0)),
            ],
            scratch_shapes=[
                pltpu.VMEM((rows, 2 * LANES), bf16),
                pltpu.VMEM((2, slots, 2 * LANES), bf16),
                pltpu.VMEM((2, slots, 2 * LANES), bf16),
                pltpu.VMEM((rows, 2 * LANES), bf16),
                pltpu.VMEM((LANES, rows), bf16),
                pltpu.VMEM((LANES, rows), bf16),
                pltpu.VMEM((LANES, slots), f32),
                pltpu.VMEM((LANES, slots), f32),
                pltpu.VMEM((q_tile, LANES), f32),
                pltpu.VMEM((2, LANES, width), f32),
                pltpu.VMEM((2, LANES, width), f32),
            ],
        ),
        out_shape=[
            jax.ShapeDtypeStruct((seqs, rows, pairs * LANES), bf16),
            jax.ShapeDtypeStruct((seqs, slots, pairs * LANES), bf16),
            jax.ShapeDtypeStruct((seqs, slots, pairs * LANES), bf16),
            jax.ShapeDtypeStruct((seqs, pairs, 2, width), f32),
        ],
        compiler_params=pltpu.CompilerParams(vmem_limit_bytes=VMEM_LIMIT),
        cost_estimate=cost(30 * pairs),
        name="attention_backward",
    )(lengths, offset, qkv, keys_of, values_of, attended, grad, extra, vector)


THRESHOLDS = (12, 16, 23, 32, 46, 64, 91)


def bucket_of(offsets):
    distance = jnp.abs(offsets)
    larger = jnp.full(offsets.shape, 8, jnp.int32)
    for threshold in THRESHOLDS:
        larger = larger + (distance >= threshold).astype(jnp.int32)
    nearby = jnp.where(distance < 8, distance, larger)
    return jnp.where(offsets > 0, 16, 0).astype(jnp.int32) + nearby


def bias_onehot(q_tile, k_tile, flip):
    width = strip_width(q_tile, k_tile)
    lane = jnp.arange(width, dtype=jnp.int32)
    lane = jnp.where(lane >= width - LANES, lane - width, lane)
    offs = lane - (q_tile + k_tile)
    if flip:
        offs = -offs
    return (bucket_of(offs)[:, None] == jnp.arange(32, dtype=jnp.int32)[None, :]).astype(f32)


from jax.sharding import PartitionSpec as P

D = 768
HEADS = 12
PAIRS = HEADS // 2
FF = 2048
BUCKETS = 32
EPSILON = 1e-06
PRECISE = lax.Precision.HIGHEST
BOTH = ("dp", "fsdp")
FF_CHUNK = 512
WO = slice(FF_CHUNK, FF_CHUNK + D)
GROUPS = (1, 2, 1, 2)
FORWARD_TILES = (1024, 512)
BACKWARD_TILES = (512, 256)


def rms_factor(values):
    return lax.rsqrt(jnp.mean(values * values, axis=-1, keepdims=True) + EPSILON)


def norm_back(grad_normed, values, factor, gain):
    scaled = grad_normed * gain
    return factor * scaled - values * (factor * factor * factor) * jnp.mean(
        scaled * values, axis=-1, keepdims=True
    )


def project_kernel(x_ref, w_ref, gain_ref, out_ref):
    x = x_ref[...].astype(f32)
    normed = (x * rms_factor(x) * gain_ref[...]).astype(bf16)
    for n in range(3):
        part = slice(n * D, (n + 1) * D)
        out_ref[:, part] = dot_nt(normed, w_ref[:, part]).astype(bf16)


def project(x, weights, gain, tile):
    tokens = x.shape[0]
    return pl.pallas_call(
        project_kernel,
        grid=(tokens // tile,),
        in_specs=[
            pl.BlockSpec((tile, D), lambda i: (i, 0)),
            pl.BlockSpec((D, 3 * D), lambda i: (0, 0)),
            pl.BlockSpec((1, D), lambda i: (0, 0)),
        ],
        out_specs=pl.BlockSpec((tile, 3 * D), lambda i: (i, 0)),
        out_shape=jax.ShapeDtypeStruct((tokens, 3 * D), bf16),
        compiler_params=pltpu.CompilerParams(vmem_limit_bytes=VMEM_LIMIT),
        cost_estimate=cost(12),
        name="project",
    )(x, weights, gain)


def ffn_kernel(
    tile, rows, away, lengths, place, x_ref, a_ref, c_ref, one_ref, two_ref, wgu_ref, gain_ref,
    own_ref, away_ref, gh_ref, ga_ref, dod_out, dgu_out, gain_out,
    dod, dgu, gain_acc, hidden_ref, nf_ref, seed_ref, out_acc, dnf_acc, sems,
):
    step = pl.program_id(0)
    steps = pl.num_programs(0)
    at = tile_at(step, place, away, steps)

    @pl.when(step == 0)
    def _():
        dod[...] = jnp.zeros_like(dod)
        dgu[...] = jnp.zeros_like(dgu)
        gain_acc[...] = jnp.zeros_like(gain_acc)

    per_seq = rows // tile
    seq = at // per_seq
    first = place[1] + (at - seq * per_seq) * tile
    position = first + lax.broadcasted_iota(jnp.int32, (tile, D), 0)
    hidden_ref[...] = x_ref[...].astype(f32) + dot_nt(a_ref[...], two_ref[:, WO])
    hidden = hidden_ref[...]
    factor = rms_factor(hidden)
    gain = gain_ref[...]
    nf_ref[...] = (hidden * factor * gain).astype(bf16)
    seed_ref[...] = jnp.where(position < lengths[seq], c_ref[...].astype(f32), 0.0).astype(bf16)
    out_acc[...] = hidden
    dnf_acc[...] = jnp.zeros_like(dnf_acc)

    for f0 in range(0, FF, FF_CHUNK):
        ff = slice(f0, f0 + FF_CHUNK)
        down = slice(D + f0, D + f0 + FF_CHUNK)
        w_down = one_ref[:, ff] if f0 < 2 * D else two_ref[:, :FF_CHUNK]
        nf, seed = nf_ref[...], seed_ref[...]
        each = wgu_ref.shape[1]
        w_gate = wgu_ref[f0 // each : (f0 + FF_CHUNK) // each, :, :D].reshape(FF_CHUNK, D)
        w_up = wgu_ref[f0 // each : (f0 + FF_CHUNK) // each, :, D:].reshape(FF_CHUNK, D)
        gate = dot_nt(nf, w_gate)
        up = dot_nt(nf, w_up)
        back = dot_nn(seed, w_down)
        square = gate * gate
        root = 0.7978845608028654
        tanh = jnp.tanh(gate * (root + (root * 0.044715) * square))
        half = 0.5 + 0.5 * tanh
        active = gate * half
        slope = half + (0.5 * gate) * (1.0 - tanh * tanh) * (root + (3.0 * root * 0.044715) * square)
        activated = (active * up).astype(bf16)
        grad_gate = (back * up * slope).astype(bf16)
        grad_up = (back * active).astype(bf16)
        out_acc[...] += dot_nt(activated, w_down)
        dnf_acc[...] += dot_nn(grad_gate, w_gate) + dot_nn(grad_up, w_up)
        dod[:, down] += dot_tn(seed, activated)
        dgu[ff, :D] += dot_tn(grad_gate, nf)
        dgu[ff, D:] += dot_tn(grad_up, nf)
    hidden = hidden_ref[...]
    factor = rms_factor(hidden)
    dnf = dnf_acc[...]
    gain_acc[...] += jnp.sum(dnf * hidden * factor, axis=0, keepdims=True)
    grad_hidden = seed_ref[...].astype(f32) + norm_back(dnf, hidden, factor, gain)
    gh_ref[...] = grad_hidden
    branch = grad_hidden.astype(bf16)
    ga_ref[...] = dot_nn(branch, two_ref[:, WO]).astype(bf16)
    dod[:, :D] += dot_tn(branch, a_ref[...])

    @pl.when(step < away)
    def _():
        away_ref[...] = out_acc[...].astype(bf16)

    @pl.when(step >= away)
    def _():
        own_ref[...] = out_acc[...]

    @pl.when(step == steps - 1)
    def _():
        gain_out[...] = gain_acc[...]
        one = pltpu.make_async_copy(dod, dod_out, sems.at[0])
        two = pltpu.make_async_copy(dgu, dgu_out, sems.at[1])
        one.start()
        two.start()
        one.wait()
        two.wait()


def tile_at(step, place, away, steps):
    if away == 0:
        return step
    return (step + away * (1 - place[0])) % steps


def away_index(away):
    return lambda i, *_: (jnp.minimum(i, max(away, 1) - 1), 0)


def own_index(away):
    return lambda i, *_: (jnp.maximum(i - away, 0), 0)


def ffn(x, attended, cotangent, w_one, w_two, rest, ff_share, gain, lengths, place, tile, rows, away):
    tokens = x.shape[0]
    steps = tokens // tile
    by_tile = lambda i, lengths, place: (tile_at(i, place, away, steps), 0)
    whole = lambda i, *_: (0, 0)
    single = pl.Buffered(1)
    return pl.pallas_call(
        functools.partial(ffn_kernel, tile, rows, away),
        grid_spec=pltpu.PrefetchScalarGridSpec(
            num_scalar_prefetch=2,
            grid=(steps,),
            in_specs=[
                pl.BlockSpec((tile, D), by_tile),
                pl.BlockSpec((tile, D), by_tile),
                pl.BlockSpec((tile, D), by_tile),
                pl.BlockSpec((D, 2 * D), whole, pipeline_mode=single),
                pl.BlockSpec((D, 2 * D), whole, pipeline_mode=single),
                pl.BlockSpec((rest.shape[0], ff_share, 2 * D), lambda i, *_: (0, 0, 0), pipeline_mode=single),
                pl.BlockSpec((1, D), whole),
            ],
            out_specs=[
                pl.BlockSpec((tile, D), own_index(away)),
                pl.BlockSpec((tile, D), away_index(away)),
                pl.BlockSpec((tile, D), by_tile),
                pl.BlockSpec((tile, D), by_tile),
                pl.BlockSpec(memory_space=pl.ANY),
                pl.BlockSpec(memory_space=pl.ANY),
                pl.BlockSpec((1, D), whole),
            ],
            scratch_shapes=[
                pltpu.VMEM((D, D + FF), f32),
                pltpu.VMEM((FF, 2 * D), f32),
                pltpu.VMEM((1, D), f32),
                pltpu.VMEM((tile, D), f32),
                pltpu.VMEM((tile, D), bf16),
                pltpu.VMEM((tile, D), bf16),
                pltpu.VMEM((tile, D), f32),
                pltpu.VMEM((tile, D), f32),
                pltpu.SemaphoreType.DMA((2,)),
            ],
        ),
        out_shape=[
            jax.ShapeDtypeStruct((tokens - away * tile, D), f32),
            jax.ShapeDtypeStruct((max(away, 1) * tile, D), bf16),
            jax.ShapeDtypeStruct((tokens, D), f32),
            jax.ShapeDtypeStruct((tokens, D), bf16),
            jax.ShapeDtypeStruct((D, D + FF), f32),
            jax.ShapeDtypeStruct((FF, 2 * D), f32),
            jax.ShapeDtypeStruct((1, D), f32),
        ],
        compiler_params=pltpu.CompilerParams(vmem_limit_bytes=VMEM_LIMIT),
        cost_estimate=cost(95),
        name="ffn",
    )(lengths, place, x, attended, cotangent, w_one, w_two, rest, gain)


def weights_kernel(pieces, x_ref, gain_ref, *refs):
    grads, dw_ref = refs[:-1], refs[-1]

    @pl.when(pl.program_id(0) == 0)
    def _():
        dw_ref[...] = jnp.zeros_like(dw_ref)

    x = x_ref[...].astype(f32)
    normed = (x * rms_factor(x) * gain_ref[...]).astype(bf16)
    for n in range(3):
        row = 0
        for ref in grads[n * pieces : (n + 1) * pieces]:
            rows = slice(row, row + ref.shape[1])
            dw_ref[rows, n * D : (n + 1) * D] += dot_tn(ref[...], normed)
            row += ref.shape[1]


def finish_weights(x, gain, dq, dk, dv, tile):
    tokens = x.shape[0]
    grads = [*dq, *dk, *dv]
    return pl.pallas_call(
        functools.partial(weights_kernel, len(dq)),
        grid=(tokens // tile,),
        in_specs=[pl.BlockSpec((tile, D), lambda i: (i, 0)), pl.BlockSpec((1, D), lambda i: (0, 0))]
        + [pl.BlockSpec((tile, g.shape[1]), lambda i: (i, 0)) for g in grads],
        out_specs=pl.BlockSpec((sum(g.shape[1] for g in dq), 3 * D), lambda i: (0, 0)),
        out_shape=jax.ShapeDtypeStruct((sum(g.shape[1] for g in dq), 3 * D), f32),
        compiler_params=pltpu.CompilerParams(vmem_limit_bytes=VMEM_LIMIT),
        cost_estimate=cost(14),
        name="finish_weights",
    )(x, gain, *grads)


def finish_kernel(away, pieces, place, x_ref, gh_ref, w_ref, gain_ref, *refs):
    grads, (own_ref, away_ref, gain_out) = refs[:-3], refs[-3:]
    step = pl.program_id(0)

    @pl.when(step == 0)
    def _():
        gain_out[...] = jnp.zeros_like(gain_out)

    grad_normed = None
    for n in range(3):
        row = 0
        for ref in grads[n * pieces : (n + 1) * pieces]:
            more = dot_nn(ref[...], w_ref[row : row + ref.shape[1], n * D : (n + 1) * D])
            grad_normed = more if grad_normed is None else grad_normed + more
            row += ref.shape[1]
    x = x_ref[...].astype(f32)
    factor = rms_factor(x)
    gain_out[...] += jnp.sum(grad_normed * x * factor, axis=0, keepdims=True)
    grad_x = gh_ref[...] + norm_back(grad_normed, x, factor, gain_ref[...])

    @pl.when(step < away)
    def _():
        away_ref[...] = grad_x.astype(bf16)

    @pl.when(step >= away)
    def _():
        own_ref[...] = grad_x


def finish_inputs(x, gh, weights, gain, dq, dk, dv, place, tile, away):
    tokens = x.shape[0]
    steps = tokens // tile
    by_tile = lambda i, place: (tile_at(i, place, away, steps), 0)
    whole = lambda i, *_: (0, 0)
    grads = [*dq, *dk, *dv]
    return pl.pallas_call(
        functools.partial(finish_kernel, away, len(dq)),
        grid_spec=pltpu.PrefetchScalarGridSpec(
            num_scalar_prefetch=1,
            grid=(steps,),
            in_specs=[
                pl.BlockSpec((tile, D), by_tile),
                pl.BlockSpec((tile, D), by_tile),
                pl.BlockSpec((D, 3 * D), whole),
                pl.BlockSpec((1, D), whole),
            ]
            + [pl.BlockSpec((tile, g.shape[1]), by_tile) for g in grads],
            out_specs=[
                pl.BlockSpec((tile, D), own_index(away)),
                pl.BlockSpec((tile, D), away_index(away)),
                pl.BlockSpec((1, D), whole),
            ],
        ),
        out_shape=[
            jax.ShapeDtypeStruct((tokens - away * tile, D), f32),
            jax.ShapeDtypeStruct((max(away, 1) * tile, D), bf16),
            jax.ShapeDtypeStruct((1, D), f32),
        ],
        compiler_params=pltpu.CompilerParams(vmem_limit_bytes=VMEM_LIMIT),
        cost_estimate=cost(16),
        name="finish_inputs",
    )(place, x, gh, weights, gain, *grads)


Y, CORE, X, Z = 1, 2, 4, 8
SQUARE_DEVICES = 32


def from_peer(value, flip):
    return lax.ppermute(value, BOTH, [(n, n ^ flip) for n in range(SQUARE_DEVICES)])


def bit(me, which):
    return (me // which) % 2


def gather_rows(shard, *alongside):
    me = lax.axis_index(BOTH)
    n, lanes = shard.shape
    z = me // Z
    parts = [shard] + [from_peer(shard, k * Z) for k in (1, 2, 3)]
    parts = after(parts, *alongside[0:1])
    column = jnp.stack([pick(parts, z ^ at) for at in range(4)])
    square = [column] + [from_peer(column, k) for k in (Y, X, X + Y)]
    square = after(square, *alongside[1:2])
    corner = bit(me, X) * 2 + bit(me, Y)
    plane = jnp.stack([pick(square, corner ^ at) for at in range(4)], axis=1).reshape(4, 2, 2, n, lanes)
    other = after(from_peer(plane, CORE), *alongside[2:3])
    core = bit(me, CORE)
    both = jnp.stack([jnp.where(core == 0, plane, other), jnp.where(core == 0, other, plane)], axis=2)
    return both.reshape(32 * n, lanes)


def pick(parts, at):
    out = parts[0]
    for n in range(1, len(parts)):
        out = jnp.where(at == n, parts[n], out)
    return out


def scatter_rows(total):
    me = lax.axis_index(BOTH)
    n, lanes = total.shape[0] // 32, total.shape[1]
    blocks = total.reshape(4, 2, 2, 2, n, lanes)
    core, x, y, z = bit(me, CORE), bit(me, X), bit(me, Y), me // Z
    take = lambda a, at, axis: lax.dynamic_index_in_dim(a, at, axis, keepdims=False)
    sent = from_peer(take(blocks, 1 - core, 2).astype(bf16), CORE)
    sent = yield sent
    mine = (take(blocks, core, 2) + sent.astype(f32)).reshape(4, 4, n, lanes)
    corner = 2 * x + y
    sent = [from_peer(take(mine, corner ^ k, 1).astype(bf16), (k // 2) * X + (k % 2) * Y) for k in (1, 2, 3)]
    sent = yield sent
    mine = take(mine, corner, 1) + (sent[0].astype(f32) + sent[1].astype(f32) + sent[2].astype(f32))
    sent = [from_peer(take(mine, z ^ k, 0).astype(bf16), k * Z) for k in (1, 2, 3)]
    sent = yield sent
    yield take(mine, z, 0) + (sent[0].astype(f32) + sent[1].astype(f32) + sent[2].astype(f32))


def scatter_plain(total):
    sent = yield total.astype(bf16)
    sent = yield sent
    sent = yield sent
    yield lax.psum_scatter(sent, BOTH, scatter_dimension=0, tiled=True).astype(f32)


def sum_all(value):
    value = value + from_peer(value, CORE)
    value = value + (from_peer(value, Y) + from_peer(value, X) + from_peer(value, X + Y))
    return value + (from_peer(value, Z) + from_peer(value, 2 * Z) + from_peer(value, 3 * Z))


def swap_start(block, side):
    other = lax.dynamic_index_in_dim(block, 1 - side, 0, keepdims=False)
    return lax.ppermute(other, "fsdp", [(0, 1), (1, 0)])


def swap_in(block, come, side):
    mine = lax.dynamic_index_in_dim(block, side, 0, keepdims=False)
    return jnp.where(side == 0, jnp.concatenate([mine, come]), jnp.concatenate([come, mine]))


def swap_out(own, come, side):
    come = come.astype(f32)
    return jnp.where(side == 0, jnp.stack([own, come]), jnp.stack([come, own]))


def turned(weight):
    return weight.astype(bf16).T


def after(value, *others):
    if not others:
        return value
    return lax.optimization_barrier((value, *others))[0]


def per_device(
    sizes, inputs, cotangent, lengths, w_query, w_key, w_value, w_out, w_gate, w_up, w_down,
    gain_attn, gain_ffn, bias_table,
):
    seqs, own_rows, _ = inputs.shape
    sides = sizes["fsdp"]
    slots = own_rows * sides
    side = lax.axis_index("fsdp")
    swap = seqs == 2 and sides == 2
    if sizes["dp"] * sides == SQUARE_DEVICES and sides == 2:
        gather, scatter, total = gather_rows, scatter_rows, sum_all
    else:
        gather = lambda a, *b: lax.all_gather(a, BOTH, axis=0, tiled=True)
        scatter = scatter_plain
        total = lambda a: lax.psum(a, BOTH)
    if swap:
        other = lax.dynamic_index_in_dim(inputs, 1 - side, 0, keepdims=False)
        other, w_query, w_key, w_value = lax.optimization_barrier((other, w_query, w_key, w_value))
        come = [lax.ppermute(part, "fsdp", [(0, 1), (1, 0)]) for part in jnp.split(other, (384, 768))]
    else:
        come = []
    gains = jnp.pad(jnp.stack([gain_attn, gain_ffn], axis=1).astype(bf16), ((0, 0), (0, LANES - 2)))
    packed = jnp.concatenate([turned(w_query), turned(w_key), turned(w_value), gains], axis=1)
    w_out, w_gate, w_up, w_down, packed = lax.optimization_barrier((w_out, w_gate, w_up, w_down, packed))
    wqkv = gather(packed, *come)
    gain_rows = wqkv[:, 3 * D : 3 * D + 2].astype(f32).T
    rest = jnp.concatenate(
        [
            jnp.concatenate([turned(w_gate), turned(w_up)], axis=1),
            turned(w_down)[:, : 2 * D],
            jnp.pad(jnp.concatenate([turned(w_down)[:, 2 * D :], turned(w_out)], axis=1), ((0, 0), (0, 256))),
        ]
    )
    rest = lax.all_gather(after(rest, wqkv), BOTH)
    share, ff_share = gain_attn.shape[0], w_gate.shape[1]
    w_one = rest[:, ff_share : ff_share + share].reshape(D, 2 * D)
    w_two = rest[:, ff_share + share :].reshape(D, 2 * D)
    if swap:
        x = swap_in(inputs, jnp.concatenate(come), side)
        lengths = lax.dynamic_slice_in_dim(lengths, side, 1)
        seqs, rows, first = 1, slots, jnp.zeros((), jnp.int32)
    else:
        x = inputs.reshape(-1, D)
        rows, first = own_rows, side * own_rows
    tile = min(512, own_rows)
    away = own_rows // tile if swap else 0
    place = jnp.stack([side, first]).astype(jnp.int32)
    origin = place[1:]
    ahead_tiles = (min(FORWARD_TILES[0], rows), FORWARD_TILES[1])
    back_tiles = (min(BACKWARD_TILES[0], rows), BACKWARD_TILES[1])
    one_hot = bias_onehot(*back_tiles, False)
    vector = jnp.dot(one_hot, bias_table, precision=PRECISE).T.reshape(PAIRS, 2, -1)
    flipped = jnp.dot(bias_onehot(*ahead_tiles, True), bias_table, precision=PRECISE).T.reshape(PAIRS, 2, -1)

    qkv = project(x, wqkv, gain_rows[0:1], tile).reshape(seqs, rows, 3 * D)
    if swap:
        cotangent = after(cotangent, x)
        seed_come = swap_start(cotangent, side)
    if rows < slots:
        kv = lax.all_gather(qkv[:, :, D:], "fsdp", axis=1, tiled=True)
        sources = (kv, kv, 0, PAIRS)
    else:
        sources = (qkv, qkv, PAIRS, 2 * PAIRS)
    attended, extra = attention_forward(qkv, sources, lengths, origin, flipped, *ahead_tiles, PAIRS)
    if swap:
        seed = swap_in(cotangent, after(seed_come, attended), side)
    else:
        seed = cotangent.reshape(-1, D)
    own, away_out, grad_hidden, grad_attended, dod, dgu, gain_two = ffn(
        x, attended.reshape(-1, D), seed, w_one, w_two, rest, ff_share, gain_rows[1:2], lengths, place, tile, rows, away
    )
    grad_attended = grad_attended.reshape(seqs, rows, D)
    dq, dk, dv, strips = [], [], [], []
    scatters = [scatter(dod), scatter(dgu)]
    moving = [next(s) for s in scatters]
    back = []
    if swap:
        back = [lax.ppermute(away_out, "fsdp", [(0, 1), (1, 0)])]
    low = 0
    for stage, group in enumerate(GROUPS):
        one, two, three, strip = attention_backward(
            qkv, sources, attended, grad_attended, extra, lengths, origin, vector, *back_tiles, low, group
        )
        if rows < slots:
            two = lax.psum_scatter(two, "fsdp", scatter_dimension=1, tiled=True)
            three = lax.psum_scatter(three, "fsdp", scatter_dimension=1, tiled=True)
        dq.append(one.reshape(-1, group * LANES))
        dk.append(two.reshape(-1, group * LANES))
        dv.append(three.reshape(-1, group * LANES))
        strips.append(strip)
        low += group
        if stage < 3:
            moving, extra, dq, dk, dv = lax.optimization_barrier((moving, extra, dq, dk, dv))
            moving = [s.send(m) for s, m in zip(scatters, moving)]
        else:
            moving, back, dq, dk, dv = lax.optimization_barrier((moving, back, dq, dk, dv))
    out_down, gate_up = moving
    if swap:
        output = swap_out(own, back[0], side)
    else:
        output = own.reshape(seqs, rows, D)
    dq = after(dq, output)
    dw = finish_weights(x, gain_rows[0:1], dq, dk, dv, tile)
    scatter_qk = scatter(dw)
    moving = next(scatter_qk)
    own, away_grad, gain_one = finish_inputs(
        x, grad_hidden, wqkv, gain_rows[0:1], after(dq, dw), dk, dv, place, tile, away
    )
    moving, own, gain_one = lax.optimization_barrier((moving, own, gain_one))
    if swap:
        back = [lax.ppermute(part, "fsdp", [(0, 1), (1, 0)]) for part in jnp.split(away_grad, 2)]
    else:
        back = [own, own]
    moving = scatter_qk.send(moving)
    diagonals = jnp.sum(jnp.concatenate(strips, axis=1), axis=0).reshape(HEADS, -1)
    table = jnp.dot(diagonals, one_hot, precision=PRECISE).T
    small = jnp.concatenate([gain_one, gain_two, jnp.pad(table.reshape(1, -1), ((0, 0), (0, D - BUCKETS * HEADS)))])
    small = total(small)
    moving, back[0], small = lax.optimization_barrier((moving, back[0], small))
    moving = scatter_qk.send(moving)
    moving, back[1] = lax.optimization_barrier((moving, back[1]))
    query_key = scatter_qk.send(moving)
    gain_shares = lax.dynamic_slice_in_dim(small[:2], lax.axis_index(BOTH) * gain_attn.shape[0], gain_attn.shape[0], 1)
    if swap:
        grad_inputs = swap_out(own, jnp.concatenate(back), side)
    else:
        grad_inputs = own.reshape(seqs, rows, D)
    return (
        output,
        grad_inputs,
        query_key[:, :D].T,
        query_key[:, D : 2 * D].T,
        query_key[:, 2 * D : 3 * D].T,
        out_down[:, :D].T,
        gate_up[:, :D].T,
        gate_up[:, D:].T,
        out_down[:, D:].T,
        gain_shares[0],
        gain_shares[1],
        small[2, : BUCKETS * HEADS].reshape(BUCKETS, HEADS),
    )


def solution(mesh):
    tokens = P("dp", "fsdp", None)
    columns = P(None, BOTH)
    return jax.shard_map(
        functools.partial(per_device, dict(mesh.shape)),
        mesh=mesh,
        in_specs=(tokens, tokens, P("dp")) + (columns,) * 7 + (P(BOTH), P(BOTH), P()),
        out_specs=(tokens, tokens) + (columns,) * 7 + (P(BOTH), P(BOTH), P()),
        check_vma=False,
    )
```

```python
import functools, jax, jax.numpy as jnp
from jax import lax
from jax.experimental import pallas as pl
from jax.experimental.pallas import tpu as pltpu

HEAD_DIM = 64
LANES = 128
SUB_TILE = 256
MASKED = -1000000000.0
VMEM_LIMIT = 60 << 20


def cost(microseconds):
    return pl.CostEstimate(flops=int(1.1e9 * microseconds), bytes_accessed=1 << 20, transcendentals=0)
f32, bf16 = jnp.float32, jnp.bfloat16


def dot_nt(a, b):
    return lax.dot_general(a, b, (((1,), (1,)), ((), ())), preferred_element_type=f32)


def dot_nn(a, b):
    return lax.dot_general(a, b, (((1,), (0,)), ((), ())), preferred_element_type=f32)


def dot_tn(a, b):
    return lax.dot_general(a, b, (((0,), (0,)), ((), ())), preferred_element_type=f32)


def three_pieces(x):
    hi = x.astype(bf16).astype(f32)
    mid = (x - hi).astype(bf16).astype(f32)
    return hi, mid, x - hi - mid


def skewed(row, width):
    spread = jnp.broadcast_to(row, (LANES, width))
    return pltpu.roll(spread, 0, 1, stride=1, stride_axis=0)


def lane_iota(rows):
    return lax.broadcasted_iota(jnp.int32, (rows, LANES), 1)


def key_extra(rows, length, ones_low, ones_high):
    lanes = lane_iota(rows)
    position = lax.broadcasted_iota(jnp.int32, (rows, LANES), 0)
    ones = ((lanes >= ones_low) & (lanes < ones_high)).astype(f32)
    masked = jnp.where(position < length, 0.0, MASKED)
    return jnp.where(lanes == 6, masked, ones).astype(bf16)


def forward_kernel(q_tile, k_tile, lengths, offset, q_ref, k_ref, v_ref, bias_ref, out_ref, extra_ref, keys, values, strips, scores_even, scores_odd):
    slots = k_ref.shape[1]
    tile = pl.program_id(2)
    origin = q_tile + k_tile
    chunks = slots // k_tile

    @pl.when(tile == 0)
    def _():
        keys[:, :LANES] = k_ref[0]
        keys[:, LANES:] = key_extra(slots, lengths[pl.program_id(0)], 0, 0)
        turned = v_ref[0].astype(f32).T.astype(bf16)
        for h in range(2):
            values[h, :HEAD_DIM, :] = turned[h * HEAD_DIM : (h + 1) * HEAD_DIM]
            values[h, HEAD_DIM:, :] = jnp.ones((16, slots), bf16)
            strips[h] = skewed(bias_ref[0, h : h + 1, :], strips.shape[2])

    lanes = lane_iota(q_tile)
    pair = q_ref[0].astype(f32)
    const = jnp.where(lanes == 6, 1.0, 0.0).astype(bf16)
    weights = [
        jnp.concatenate([jnp.where((lanes < HEAD_DIM) == (h == 0), pair, 0.0).astype(bf16), const], axis=1)
        for h in range(2)
    ]
    first = offset[0] + tile * q_tile
    sub = min(SUB_TILE, q_tile)
    chains = [(u, h) for u in range(q_tile // sub) for h in range(2)]
    scores = (scores_even, scores_odd)
    tops, totals = {}, {}
    for n in range(len(chains) + 1):
        top = jnp.full((8, sub), -jnp.inf, f32)
        total = jnp.zeros((HEAD_DIM + 16, sub), f32)
        for c in range(chunks):
            rows = slice(c * k_tile, (c + 1) * k_tile)
            if n < len(chains):
                u, h = chains[n]
                raw = dot_nt(keys[rows, :], weights[h][u * sub : (u + 1) * sub])
                base = jnp.clip(c * k_tile - first - u * sub, -(k_tile + LANES), q_tile + LANES)
                for b in range(k_tile // LANES):
                    at = pl.multiple_of(origin - base - b * LANES, LANES)
                    part = raw[b * LANES : (b + 1) * LANES] + strips[h, :, pl.ds(at, sub)]
                    scores[n % 2][c * k_tile + b * LANES : c * k_tile + (b + 1) * LANES, :] = part
                    top = jnp.maximum(top, jnp.max(part.reshape(LANES // 8, 8, sub), axis=0))
            if n > 0:
                weight = jnp.exp(scores[(n - 1) % 2][rows, :] - tops[n - 1]).astype(bf16)
                total += dot_nn(values[chains[n - 1][1], :, rows], weight)
        tops[n] = jnp.max(top, axis=0, keepdims=True)
        totals[n - 1] = total
    top = [jnp.concatenate([tops[n] for n in range(h, len(chains), 2)], axis=1) for h in range(2)]
    totals = [jnp.concatenate([totals[n] for n in range(h, len(chains), 2)], axis=1) for h in range(2)]
    mixed, pieces = [], []
    for h in range(2):
        total = totals[h][HEAD_DIM : HEAD_DIM + 1]
        mixed.append(totals[h][:HEAD_DIM] / total)
        pieces += list(three_pieces(-(top[h] + jnp.log(total))))
    out_ref[0] = jnp.concatenate(mixed, axis=0).T.astype(bf16)
    rows = lax.broadcasted_iota(jnp.int32, (LANES, q_tile), 0)
    stats = jnp.where(rows == 6, 1.0, 0.0)
    for n, piece in enumerate(pieces):
        stats = jnp.where(rows == n, piece, stats)
    extra_ref[0, 0] = stats.T.astype(bf16)


def strip_width(q_tile, k_tile):
    return 2 * (q_tile + k_tile) + 2 * LANES


def attention_forward(qkv, kv, lengths, offset, vector, q_tile, k_tile, pairs):
    seqs, rows, _ = qkv.shape
    keys_of, values_of, k_at, v_at = kv
    slots = keys_of.shape[1]
    width = strip_width(q_tile, k_tile)
    grid = (seqs, pairs, rows // q_tile)
    return pl.pallas_call(
        functools.partial(forward_kernel, q_tile, k_tile),
        grid_spec=pltpu.PrefetchScalarGridSpec(
            num_scalar_prefetch=2,
            grid=grid,
            in_specs=[
                pl.BlockSpec((1, q_tile, LANES), lambda s, p, i, *_: (s, i, p)),
                pl.BlockSpec((1, slots, LANES), lambda s, p, i, *_: (s, 0, p + k_at)),
                pl.BlockSpec((1, slots, LANES), lambda s, p, i, *_: (s, 0, p + v_at)),
                pl.BlockSpec((1, 2, width), lambda s, p, i, *_: (p, 0, 0)),
            ],
            out_specs=[
                pl.BlockSpec((1, q_tile, LANES), lambda s, p, i, *_: (s, i, p)),
                pl.BlockSpec((1, 1, q_tile, LANES), lambda s, p, i, *_: (s, p, i, 0)),
            ],
            scratch_shapes=[
                pltpu.VMEM((slots, 2 * LANES), bf16),
                pltpu.VMEM((2, HEAD_DIM + 16, slots), bf16),
                pltpu.VMEM((2, LANES, width), f32),
                pltpu.VMEM((slots, min(SUB_TILE, q_tile)), f32),
                pltpu.VMEM((slots, min(SUB_TILE, q_tile)), f32),
            ],
        ),
        out_shape=[
            jax.ShapeDtypeStruct((seqs, rows, pairs * LANES), bf16),
            jax.ShapeDtypeStruct((seqs, pairs, rows, LANES), bf16),
        ],
        compiler_params=pltpu.CompilerParams(vmem_limit_bytes=VMEM_LIMIT),
        cost_estimate=cost(100),
        name="attention_forward",
    )(lengths, offset, qkv, keys_of, values_of, vector)


def backward_kernel(
    q_tile, k_tile, lengths, offset, q_ref, k_ref, v_ref, a_ref, d_ref, extra_ref, bias_ref,
    dq_ref, dk_ref, dv_ref, bias_out,
    qa, ka, va, da, q_turned, d_turned, dk_acc, dv_acc, dq_acc, strips, sums,
):
    rows, slots = q_ref.shape[1], k_ref.shape[1]
    origin = q_tile + k_tile
    width = strips.shape[2]
    chunks = slots // k_tile
    length = lengths[pl.program_id(0)]
    lanes_k, lanes_q = lane_iota(slots), lane_iota(rows)
    half = lax.broadcasted_iota(jnp.int32, (1, LANES), 1) < HEAD_DIM
    for h in range(2):
        mine = (half == (h == 0)).astype(f32).astype(bf16)
        ka[h, :, :LANES] = k_ref[0] * mine
        ka[h, :, LANES:] = key_extra(slots, length, 3 * h, 3 * h + 3)
        va[h, :, :LANES] = v_ref[0] * mine
        va[h, :, LANES:] = ((lanes_k >= 3 * h) & (lanes_k < 3 * h + 3)).astype(f32).astype(bf16)
        strips[h] = skewed(bias_ref[0, h : h + 1, :], width)
    qa[:, :LANES] = q_ref[0]
    qa[:, LANES:] = extra_ref[0, 0]
    grads = d_ref[0].astype(f32)
    product = grads * a_ref[0].astype(f32)
    hi = product.astype(bf16)
    low = (product - hi.astype(f32)).astype(bf16)
    row_at = lax.broadcasted_iota(jnp.int32, (LANES, LANES), 0)
    lane_at = lax.broadcasted_iota(jnp.int32, (LANES, LANES), 1)
    pick = jnp.where((lane_at < 6) & ((row_at < HEAD_DIM) == (lane_at < 3)), -1.0, 0.0).astype(bf16)
    minus_dot = dot_nn(hi, pick) + dot_nn(low, pick)
    one, two, three = three_pieces(minus_dot)
    which = lanes_q % 3
    da[:, :LANES] = d_ref[0]
    da[:, LANES:] = jnp.where(which == 0, one, jnp.where(which == 1, two, three)).astype(bf16)
    q_turned[...] = q_ref[0].T
    d_turned[...] = d_ref[0].T
    dk_acc[...] = jnp.zeros_like(dk_acc)
    dv_acc[...] = jnp.zeros_like(dv_acc)
    sums[...] = jnp.zeros_like(sums)

    def one_tile(i, carried):
        r0 = pl.multiple_of(i * q_tile, q_tile)
        units = [(c, h) for c in range(chunks) for h in range(2)]

        def products(c, h):
            cols = slice(c * k_tile, (c + 1) * k_tile)
            raw = dot_nt(qa[pl.ds(r0, q_tile), :], ka[h, cols, :])
            back = dot_nt(da[pl.ds(r0, q_tile), :], va[h, cols, :])
            return raw, back

        ahead = products(*units[0])
        for n, (c, h) in enumerate(units):
            raw, back = ahead
            if n + 1 < len(units):
                ahead = products(*units[n + 1])
            base = jnp.clip(c * k_tile - offset[0] - r0, -(k_tile + LANES), q_tile + LANES)
            cols = slice(c * k_tile, (c + 1) * k_tile)
            own = slice(h * HEAD_DIM, (h + 1) * HEAD_DIM)
            probs, grad = [], []
            for b in range(q_tile // LANES):
                at = pl.multiple_of(origin + base - b * LANES, LANES)
                part = slice(b * LANES, (b + 1) * LANES)
                p = jnp.exp(raw[part] + strips[h, :, pl.ds(at, k_tile)])
                g = p * back[part]
                sums[h, :, pl.ds(at, k_tile)] += g
                probs.append(p.astype(bf16))
                grad.append(g.astype(bf16))
            probs = jnp.concatenate(probs, axis=0)
            grad = jnp.concatenate(grad, axis=0)
            dv_acc[own, cols] += dot_nn(d_turned[own, pl.ds(r0, q_tile)], probs)
            dk_acc[own, cols] += dot_nn(q_turned[own, pl.ds(r0, q_tile)], grad)
            dq = dot_nn(grad, ka[h, cols, :LANES])
            if n == 0:
                dq_acc[...] = dq
            else:
                dq_acc[...] += dq
        dq_ref[0, pl.ds(r0, q_tile), :] = dq_acc[...].astype(bf16)
        return carried

    lax.fori_loop(0, rows // q_tile, one_tile, 0)
    dk_ref[0] = dk_acc[...].T.astype(bf16)
    dv_ref[0] = dv_acc[...].T.astype(bf16)
    mirror = (row_at + lane_at == LANES - 1).astype(f32)
    for h in range(2):
        flipped = lax.dot_general(
            mirror, sums[h], (((1,), (0,)), ((), ())),
            precision=lax.Precision.HIGHEST, preferred_element_type=f32,
        )
        turned = pltpu.roll(flipped, width - (LANES - 1), 1, stride=1, stride_axis=0)
        bias_out[0, 0, h : h + 1, :] = jnp.sum(turned, axis=0, keepdims=True)


def attention_backward(qkv, kv, attended, grad, extra, lengths, offset, vector, q_tile, k_tile, low, pairs):
    seqs, rows, _ = qkv.shape
    keys_of, values_of, k_at, v_at = kv
    slots = keys_of.shape[1]
    width = strip_width(q_tile, k_tile)
    pair_of = lambda at: lambda s, p, *_: (s, 0, p + at)
    spec = lambda r, at: pl.BlockSpec((1, r, LANES), pair_of(at))
    return pl.pallas_call(
        functools.partial(backward_kernel, q_tile, k_tile),
        grid_spec=pltpu.PrefetchScalarGridSpec(
            num_scalar_prefetch=2,
            grid=(seqs, pairs),
            in_specs=[
                spec(rows, low), spec(slots, k_at + low), spec(slots, v_at + low), spec(rows, low), spec(rows, low),
                pl.BlockSpec((1, 1, rows, LANES), lambda s, p, *_: (s, p + low, 0, 0)),
                pl.BlockSpec((1, 2, width), lambda s, p, *_: (p + low, 0, 0)),
            ],
            out_specs=[
                spec(rows, 0), spec(slots, 0), spec(slots, 0),
                pl.BlockSpec((1, 1, 2, width), lambda s, p, *_: (s, p, 0, 0)),
            ],
            scratch_shapes=[
                pltpu.VMEM((rows, 2 * LANES), bf16),
                pltpu.VMEM((2, slots, 2 * LANES), bf16),
                pltpu.VMEM((2, slots, 2 * LANES), bf16),
                pltpu.VMEM((rows, 2 * LANES), bf16),
                pltpu.VMEM((LANES, rows), bf16),
                pltpu.VMEM((LANES, rows), bf16),
                pltpu.VMEM((LANES, slots), f32),
                pltpu.VMEM((LANES, slots), f32),
                pltpu.VMEM((q_tile, LANES), f32),
                pltpu.VMEM((2, LANES, width), f32),
                pltpu.VMEM((2, LANES, width), f32),
            ],
        ),
        out_shape=[
            jax.ShapeDtypeStruct((seqs, rows, pairs * LANES), bf16),
            jax.ShapeDtypeStruct((seqs, slots, pairs * LANES), bf16),
            jax.ShapeDtypeStruct((seqs, slots, pairs * LANES), bf16),
            jax.ShapeDtypeStruct((seqs, pairs, 2, width), f32),
        ],
        compiler_params=pltpu.CompilerParams(vmem_limit_bytes=VMEM_LIMIT),
        cost_estimate=cost(30 * pairs),
        name="attention_backward",
    )(lengths, offset, qkv, keys_of, values_of, attended, grad, extra, vector)


THRESHOLDS = (12, 16, 23, 32, 46, 64, 91)


def bucket_of(offsets):
    distance = jnp.abs(offsets)
    larger = jnp.full(offsets.shape, 8, jnp.int32)
    for threshold in THRESHOLDS:
        larger = larger + (distance >= threshold).astype(jnp.int32)
    nearby = jnp.where(distance < 8, distance, larger)
    return jnp.where(offsets > 0, 16, 0).astype(jnp.int32) + nearby


def bias_onehot(q_tile, k_tile, flip):
    width = strip_width(q_tile, k_tile)
    lane = jnp.arange(width, dtype=jnp.int32)
    lane = jnp.where(lane >= width - LANES, lane - width, lane)
    offs = lane - (q_tile + k_tile)
    if flip:
        offs = -offs
    return (bucket_of(offs)[:, None] == jnp.arange(32, dtype=jnp.int32)[None, :]).astype(f32)


from jax.sharding import PartitionSpec as P

D = 768
HEADS = 12
PAIRS = HEADS // 2
FF = 2048
BUCKETS = 32
EPSILON = 1e-06
PRECISE = lax.Precision.HIGHEST
BOTH = ("dp", "fsdp")
FF_CHUNK = 512
WO = slice(FF_CHUNK, FF_CHUNK + D)
GROUPS = (1, 2, 1, 2)
FORWARD_TILES = (1024, 512)
BACKWARD_TILES = (512, 256)


def rms_factor(values):
    return lax.rsqrt(jnp.mean(values * values, axis=-1, keepdims=True) + EPSILON)


def norm_back(grad_normed, values, factor, gain):
    scaled = grad_normed * gain
    return factor * scaled - values * (factor * factor * factor) * jnp.mean(
        scaled * values, axis=-1, keepdims=True
    )


def project_kernel(x_ref, w_ref, gain_ref, out_ref):
    x = x_ref[...].astype(f32)
    normed = (x * rms_factor(x) * gain_ref[...]).astype(bf16)
    for n in range(3):
        part = slice(n * D, (n + 1) * D)
        out_ref[:, part] = dot_nt(normed, w_ref[:, part]).astype(bf16)


def project(x, weights, gain, tile):
    tokens = x.shape[0]
    return pl.pallas_call(
        project_kernel,
        grid=(tokens // tile,),
        in_specs=[
            pl.BlockSpec((tile, D), lambda i: (i, 0)),
            pl.BlockSpec((D, 3 * D), lambda i: (0, 0)),
            pl.BlockSpec((1, D), lambda i: (0, 0)),
        ],
        out_specs=pl.BlockSpec((tile, 3 * D), lambda i: (i, 0)),
        out_shape=jax.ShapeDtypeStruct((tokens, 3 * D), bf16),
        compiler_params=pltpu.CompilerParams(vmem_limit_bytes=VMEM_LIMIT),
        cost_estimate=cost(12),
        name="project",
    )(x, weights, gain)


def ffn_kernel(
    tile, rows, away, lengths, place, x_ref, a_ref, c_ref, one_ref, two_ref, wgu_ref, gain_ref,
    own_ref, away_ref, gh_ref, ga_ref, dod_out, dgu_out, gain_out,
    dod, dgu, gain_acc, hidden_ref, nf_ref, seed_ref, out_acc, dnf_acc, sems,
):
    step = pl.program_id(0)
    steps = pl.num_programs(0)
    at = tile_at(step, place, away, steps)

    @pl.when(step == 0)
    def _():
        dod[...] = jnp.zeros_like(dod)
        dgu[...] = jnp.zeros_like(dgu)
        gain_acc[...] = jnp.zeros_like(gain_acc)

    per_seq = rows // tile
    seq = at // per_seq
    first = place[1] + (at - seq * per_seq) * tile
    position = first + lax.broadcasted_iota(jnp.int32, (tile, D), 0)
    hidden_ref[...] = x_ref[...].astype(f32) + dot_nt(a_ref[...], two_ref[:, WO])
    hidden = hidden_ref[...]
    factor = rms_factor(hidden)
    gain = gain_ref[...]
    nf_ref[...] = (hidden * factor * gain).astype(bf16)
    seed_ref[...] = jnp.where(position < lengths[seq], c_ref[...].astype(f32), 0.0).astype(bf16)
    out_acc[...] = hidden
    dnf_acc[...] = jnp.zeros_like(dnf_acc)

    for f0 in range(0, FF, FF_CHUNK):
        ff = slice(f0, f0 + FF_CHUNK)
        down = slice(D + f0, D + f0 + FF_CHUNK)
        w_down = one_ref[:, ff] if f0 < 2 * D else two_ref[:, :FF_CHUNK]
        nf, seed = nf_ref[...], seed_ref[...]
        each = wgu_ref.shape[1]
        w_gate = wgu_ref[f0 // each : (f0 + FF_CHUNK) // each, :, :D].reshape(FF_CHUNK, D)
        w_up = wgu_ref[f0 // each : (f0 + FF_CHUNK) // each, :, D:].reshape(FF_CHUNK, D)
        gate = dot_nt(nf, w_gate)
        up = dot_nt(nf, w_up)
        back = dot_nn(seed, w_down)
        square = gate * gate
        root = 0.7978845608028654
        tanh = jnp.tanh(gate * (root + (root * 0.044715) * square))
        half = 0.5 + 0.5 * tanh
        active = gate * half
        slope = half + (0.5 * gate) * (1.0 - tanh * tanh) * (root + (3.0 * root * 0.044715) * square)
        activated = (active * up).astype(bf16)
        grad_gate = (back * up * slope).astype(bf16)
        grad_up = (back * active).astype(bf16)
        out_acc[...] += dot_nt(activated, w_down)
        dnf_acc[...] += dot_nn(grad_gate, w_gate) + dot_nn(grad_up, w_up)
        dod[:, down] += dot_tn(seed, activated)
        dgu[ff, :D] += dot_tn(grad_gate, nf)
        dgu[ff, D:] += dot_tn(grad_up, nf)
    hidden = hidden_ref[...]
    factor = rms_factor(hidden)
    dnf = dnf_acc[...]
    gain_acc[...] += jnp.sum(dnf * hidden * factor, axis=0, keepdims=True)
    grad_hidden = seed_ref[...].astype(f32) + norm_back(dnf, hidden, factor, gain)
    gh_ref[...] = grad_hidden
    branch = grad_hidden.astype(bf16)
    ga_ref[...] = dot_nn(branch, two_ref[:, WO]).astype(bf16)
    dod[:, :D] += dot_tn(branch, a_ref[...])

    @pl.when(step < away)
    def _():
        away_ref[...] = out_acc[...].astype(bf16)

    @pl.when(step >= away)
    def _():
        own_ref[...] = out_acc[...]

    @pl.when(step == steps - 1)
    def _():
        gain_out[...] = gain_acc[...]
        one = pltpu.make_async_copy(dod, dod_out, sems.at[0])
        two = pltpu.make_async_copy(dgu, dgu_out, sems.at[1])
        one.start()
        two.start()
        one.wait()
        two.wait()


def tile_at(step, place, away, steps):
    if away == 0:
        return step
    return (step + away * (1 - place[0])) % steps


def away_index(away):
    return lambda i, *_: (jnp.minimum(i, max(away, 1) - 1), 0)


def own_index(away):
    return lambda i, *_: (jnp.maximum(i - away, 0), 0)


def ffn(x, attended, cotangent, w_one, w_two, rest, ff_share, gain, lengths, place, tile, rows, away):
    tokens = x.shape[0]
    steps = tokens // tile
    by_tile = lambda i, lengths, place: (tile_at(i, place, away, steps), 0)
    whole = lambda i, *_: (0, 0)
    single = pl.Buffered(1)
    return pl.pallas_call(
        functools.partial(ffn_kernel, tile, rows, away),
        grid_spec=pltpu.PrefetchScalarGridSpec(
            num_scalar_prefetch=2,
            grid=(steps,),
            in_specs=[
                pl.BlockSpec((tile, D), by_tile),
                pl.BlockSpec((tile, D), by_tile),
                pl.BlockSpec((tile, D), by_tile),
                pl.BlockSpec((D, 2 * D), whole, pipeline_mode=single),
                pl.BlockSpec((D, 2 * D), whole, pipeline_mode=single),
                pl.BlockSpec((rest.shape[0], ff_share, 2 * D), lambda i, *_: (0, 0, 0), pipeline_mode=single),
                pl.BlockSpec((1, D), whole),
            ],
            out_specs=[
                pl.BlockSpec((tile, D), own_index(away)),
                pl.BlockSpec((tile, D), away_index(away)),
                pl.BlockSpec((tile, D), by_tile),
                pl.BlockSpec((tile, D), by_tile),
                pl.BlockSpec(memory_space=pl.ANY),
                pl.BlockSpec(memory_space=pl.ANY),
                pl.BlockSpec((1, D), whole),
            ],
            scratch_shapes=[
                pltpu.VMEM((D, D + FF), f32),
                pltpu.VMEM((FF, 2 * D), f32),
                pltpu.VMEM((1, D), f32),
                pltpu.VMEM((tile, D), f32),
                pltpu.VMEM((tile, D), bf16),
                pltpu.VMEM((tile, D), bf16),
                pltpu.VMEM((tile, D), f32),
                pltpu.VMEM((tile, D), f32),
                pltpu.SemaphoreType.DMA((2,)),
            ],
        ),
        out_shape=[
            jax.ShapeDtypeStruct((tokens - away * tile, D), f32),
            jax.ShapeDtypeStruct((max(away, 1) * tile, D), bf16),
            jax.ShapeDtypeStruct((tokens, D), f32),
            jax.ShapeDtypeStruct((tokens, D), bf16),
            jax.ShapeDtypeStruct((D, D + FF), f32),
            jax.ShapeDtypeStruct((FF, 2 * D), f32),
            jax.ShapeDtypeStruct((1, D), f32),
        ],
        compiler_params=pltpu.CompilerParams(vmem_limit_bytes=VMEM_LIMIT),
        cost_estimate=cost(95),
        name="ffn",
    )(lengths, place, x, attended, cotangent, w_one, w_two, rest, gain)


def weights_kernel(pieces, x_ref, gain_ref, w_ref, *refs):
    grads, (dw_ref, gain_out) = refs[:-2], refs[-2:]

    @pl.when(pl.program_id(0) == 0)
    def _():
        dw_ref[...] = jnp.zeros_like(dw_ref)

    x = x_ref[...].astype(f32)
    normed = (x * rms_factor(x) * gain_ref[...]).astype(bf16)
    for n in range(3):
        row = 0
        for ref in grads[n * pieces : (n + 1) * pieces]:
            rows = slice(row, row + ref.shape[1])
            dw_ref[rows, n * D : (n + 1) * D] += dot_tn(ref[...], normed)
            row += ref.shape[1]

    @pl.when(pl.program_id(0) == pl.num_programs(0) - 1)
    def _():
        together = 0.0
        for n in range(3):
            part = slice(n * D, (n + 1) * D)
            together += jnp.sum(dw_ref[:, part] * w_ref[:, part].astype(f32), axis=0, keepdims=True)
        gain_out[...] = together / gain_ref[...]


def finish_weights(x, gain, weights, dq, dk, dv, tile):
    tokens = x.shape[0]
    grads = [*dq, *dk, *dv]
    return pl.pallas_call(
        functools.partial(weights_kernel, len(dq)),
        grid=(tokens // tile,),
        in_specs=[
            pl.BlockSpec((tile, D), lambda i: (i, 0)),
            pl.BlockSpec((1, D), lambda i: (0, 0)),
            pl.BlockSpec((D, 3 * D), lambda i: (0, 0)),
        ]
        + [pl.BlockSpec((tile, g.shape[1]), lambda i: (i, 0)) for g in grads],
        out_specs=[pl.BlockSpec((D, 3 * D), lambda i: (0, 0)), pl.BlockSpec((1, D), lambda i: (0, 0))],
        out_shape=[jax.ShapeDtypeStruct((D, 3 * D), f32), jax.ShapeDtypeStruct((1, D), f32)],
        compiler_params=pltpu.CompilerParams(vmem_limit_bytes=VMEM_LIMIT),
        cost_estimate=cost(14),
        name="finish_weights",
    )(x, gain, weights, *grads)


def finish_kernel(away, pieces, place, x_ref, gh_ref, w_ref, gain_ref, *refs):
    grads, (own_ref, away_ref) = refs[:-2], refs[-2:]
    step = pl.program_id(0)

    grad_normed = None
    for n in range(3):
        row = 0
        for ref in grads[n * pieces : (n + 1) * pieces]:
            more = dot_nn(ref[...], w_ref[row : row + ref.shape[1], n * D : (n + 1) * D])
            grad_normed = more if grad_normed is None else grad_normed + more
            row += ref.shape[1]
    x = x_ref[...].astype(f32)
    factor = rms_factor(x)
    grad_x = gh_ref[...] + norm_back(grad_normed, x, factor, gain_ref[...])

    @pl.when(step < away)
    def _():
        away_ref[...] = grad_x.astype(bf16)

    @pl.when(step >= away)
    def _():
        own_ref[...] = grad_x


def finish_inputs(x, gh, weights, gain, dq, dk, dv, place, tile, away):
    tokens = x.shape[0]
    steps = tokens // tile
    by_tile = lambda i, place: (tile_at(i, place, away, steps), 0)
    whole = lambda i, *_: (0, 0)
    grads = [*dq, *dk, *dv]
    return pl.pallas_call(
        functools.partial(finish_kernel, away, len(dq)),
        grid_spec=pltpu.PrefetchScalarGridSpec(
            num_scalar_prefetch=1,
            grid=(steps,),
            in_specs=[
                pl.BlockSpec((tile, D), by_tile),
                pl.BlockSpec((tile, D), by_tile),
                pl.BlockSpec((D, 3 * D), whole),
                pl.BlockSpec((1, D), whole),
            ]
            + [pl.BlockSpec((tile, g.shape[1]), by_tile) for g in grads],
            out_specs=[
                pl.BlockSpec((tile, D), own_index(away)),
                pl.BlockSpec((tile, D), away_index(away)),
            ],
        ),
        out_shape=[
            jax.ShapeDtypeStruct((tokens - away * tile, D), f32),
            jax.ShapeDtypeStruct((max(away, 1) * tile, D), bf16),
        ],
        compiler_params=pltpu.CompilerParams(vmem_limit_bytes=VMEM_LIMIT),
        cost_estimate=cost(16),
        name="finish_inputs",
    )(place, x, gh, weights, gain, *grads)


Y, CORE, X, Z = 1, 2, 4, 8
SQUARE_DEVICES = 32


def from_peer(value, flip):
    return lax.ppermute(value, BOTH, [(n, n ^ flip) for n in range(SQUARE_DEVICES)])


def bit(me, which):
    return (me // which) % 2


def gather_rows(shard, *alongside):
    me = lax.axis_index(BOTH)
    n, lanes = shard.shape
    z = me // Z
    parts = [shard] + [from_peer(shard, k * Z) for k in (1, 2, 3)]
    parts = after(parts, *alongside[0:1])
    column = jnp.stack([pick(parts, z ^ at) for at in range(4)])
    square = [column] + [from_peer(column, k) for k in (Y, X, X + Y)]
    square = after(square, *alongside[1:2])
    corner = bit(me, X) * 2 + bit(me, Y)
    plane = jnp.stack([pick(square, corner ^ at) for at in range(4)], axis=1).reshape(4, 2, 2, n, lanes)
    other = after(from_peer(plane, CORE), *alongside[2:3])
    core = bit(me, CORE)
    both = jnp.stack([jnp.where(core == 0, plane, other), jnp.where(core == 0, other, plane)], axis=2)
    return both.reshape(32 * n, lanes)


def pick(parts, at):
    out = parts[0]
    for n in range(1, len(parts)):
        out = jnp.where(at == n, parts[n], out)
    return out


def scatter_rows(total):
    me = lax.axis_index(BOTH)
    n, lanes = total.shape[0] // 32, total.shape[1]
    blocks = total.reshape(4, 2, 2, 2, n, lanes)
    core, x, y, z = bit(me, CORE), bit(me, X), bit(me, Y), me // Z
    take = lambda a, at, axis: lax.dynamic_index_in_dim(a, at, axis, keepdims=False)
    sent = from_peer(take(blocks, 1 - core, 2).astype(bf16), CORE)
    sent = yield sent
    mine = (take(blocks, core, 2) + sent.astype(f32)).reshape(4, 4, n, lanes)
    corner = 2 * x + y
    sent = [from_peer(take(mine, corner ^ k, 1).astype(bf16), (k // 2) * X + (k % 2) * Y) for k in (1, 2, 3)]
    sent = yield sent
    mine = take(mine, corner, 1) + (sent[0].astype(f32) + sent[1].astype(f32) + sent[2].astype(f32))
    sent = [from_peer(take(mine, z ^ k, 0).astype(bf16), k * Z) for k in (1, 2, 3)]
    sent = yield sent
    yield take(mine, z, 0) + (sent[0].astype(f32) + sent[1].astype(f32) + sent[2].astype(f32))


def scatter_plain(total):
    sent = yield total.astype(bf16)
    sent = yield sent
    sent = yield sent
    yield lax.psum_scatter(sent, BOTH, scatter_dimension=0, tiled=True).astype(f32)


def sum_all(value):
    value = value + from_peer(value, CORE)
    value = value + (from_peer(value, Z) + from_peer(value, 2 * Z) + from_peer(value, 3 * Z))
    return value + (from_peer(value, Y) + from_peer(value, X) + from_peer(value, X + Y))


def swap_start(block, side):
    other = lax.dynamic_index_in_dim(block, 1 - side, 0, keepdims=False)
    return lax.ppermute(other, "fsdp", [(0, 1), (1, 0)])


def swap_in(block, come, side):
    mine = lax.dynamic_index_in_dim(block, side, 0, keepdims=False)
    return jnp.where(side == 0, jnp.concatenate([mine, come]), jnp.concatenate([come, mine]))


def swap_out(own, come, side):
    come = come.astype(f32)
    return jnp.where(side == 0, jnp.stack([own, come]), jnp.stack([come, own]))


def turned(weight):
    return weight.astype(bf16).T


def after(value, *others):
    if not others:
        return value
    return lax.optimization_barrier((value, *others))[0]


def per_device(
    sizes, inputs, cotangent, lengths, w_query, w_key, w_value, w_out, w_gate, w_up, w_down,
    gain_attn, gain_ffn, bias_table,
):
    seqs, own_rows, _ = inputs.shape
    sides = sizes["fsdp"]
    slots = own_rows * sides
    side = lax.axis_index("fsdp")
    swap = seqs == 2 and sides == 2
    if sizes["dp"] * sides == SQUARE_DEVICES and sides == 2:
        gather, scatter, total = gather_rows, scatter_rows, sum_all
    else:
        gather = lambda a, *b: lax.all_gather(a, BOTH, axis=0, tiled=True)
        scatter = scatter_plain
        total = lambda a: lax.psum(a, BOTH)
    if swap:
        other = lax.dynamic_index_in_dim(inputs, 1 - side, 0, keepdims=False)
        other, w_query, w_key, w_value = lax.optimization_barrier((other, w_query, w_key, w_value))
        come = [lax.ppermute(part, "fsdp", [(0, 1), (1, 0)]) for part in jnp.split(other, (384, 768))]
    else:
        come = []
    gains = jnp.pad(jnp.stack([gain_attn, gain_ffn], axis=1).astype(bf16), ((0, 0), (0, LANES - 2)))
    packed = jnp.concatenate([turned(w_query), turned(w_key), turned(w_value), gains], axis=1)
    w_out, w_gate, w_up, w_down, packed = lax.optimization_barrier((w_out, w_gate, w_up, w_down, packed))
    wqkv = gather(packed, *come)
    gain_rows = wqkv[:, 3 * D : 3 * D + 2].astype(f32).T
    rest = jnp.concatenate(
        [
            jnp.concatenate([turned(w_gate), turned(w_up)], axis=1),
            turned(w_down)[:, : 2 * D],
            jnp.pad(jnp.concatenate([turned(w_down)[:, 2 * D :], turned(w_out)], axis=1), ((0, 0), (0, 256))),
        ]
    )
    rest = lax.all_gather(after(rest, wqkv), BOTH)
    share, ff_share = gain_attn.shape[0], w_gate.shape[1]
    w_one = rest[:, ff_share : ff_share + share].reshape(D, 2 * D)
    w_two = rest[:, ff_share + share :].reshape(D, 2 * D)
    if swap:
        x = swap_in(inputs, jnp.concatenate(come), side)
        lengths = lax.dynamic_slice_in_dim(lengths, side, 1)
        seqs, rows, first = 1, slots, jnp.zeros((), jnp.int32)
    else:
        x = inputs.reshape(-1, D)
        rows, first = own_rows, side * own_rows
    tile = min(512, own_rows)
    away = own_rows // tile if swap else 0
    place = jnp.stack([side, first]).astype(jnp.int32)
    origin = place[1:]
    ahead_tiles = (min(FORWARD_TILES[0], rows), FORWARD_TILES[1])
    back_tiles = (min(BACKWARD_TILES[0], rows), BACKWARD_TILES[1])
    one_hot = bias_onehot(*back_tiles, False)
    vector = jnp.dot(one_hot, bias_table, precision=PRECISE).T.reshape(PAIRS, 2, -1)
    flipped = jnp.dot(bias_onehot(*ahead_tiles, True), bias_table, precision=PRECISE).T.reshape(PAIRS, 2, -1)

    qkv = project(x, wqkv, gain_rows[0:1], tile).reshape(seqs, rows, 3 * D)
    if swap:
        cotangent = after(cotangent, x)
        seed_come = swap_start(cotangent, side)
    if rows < slots:
        kv = lax.all_gather(qkv[:, :, D:], "fsdp", axis=1, tiled=True)
        sources = (kv, kv, 0, PAIRS)
    else:
        sources = (qkv, qkv, PAIRS, 2 * PAIRS)
    attended, extra = attention_forward(qkv, sources, lengths, origin, flipped, *ahead_tiles, PAIRS)
    if swap:
        seed = swap_in(cotangent, after(seed_come, attended), side)
    else:
        seed = cotangent.reshape(-1, D)
    own, away_out, grad_hidden, grad_attended, dod, dgu, gain_two = ffn(
        x, attended.reshape(-1, D), seed, w_one, w_two, rest, ff_share, gain_rows[1:2], lengths, place, tile, rows, away
    )
    grad_attended = grad_attended.reshape(seqs, rows, D)
    dq, dk, dv, strips = [], [], [], []
    scatters = [scatter(dod), scatter(dgu)]
    moving = [next(s) for s in scatters]
    back = []
    if swap:
        back = [lax.ppermute(away_out, "fsdp", [(0, 1), (1, 0)])]
    low = 0
    for stage, group in enumerate(GROUPS):
        one, two, three, strip = attention_backward(
            qkv, sources, attended, grad_attended, extra, lengths, origin, vector, *back_tiles, low, group
        )
        if rows < slots:
            two = lax.psum_scatter(two, "fsdp", scatter_dimension=1, tiled=True)
            three = lax.psum_scatter(three, "fsdp", scatter_dimension=1, tiled=True)
        dq.append(one.reshape(-1, group * LANES))
        dk.append(two.reshape(-1, group * LANES))
        dv.append(three.reshape(-1, group * LANES))
        strips.append(strip)
        low += group
        if stage < 3:
            moving, extra, dq, dk, dv = lax.optimization_barrier((moving, extra, dq, dk, dv))
            moving = [s.send(m) for s, m in zip(scatters, moving)]
        else:
            moving, back, dq, dk, dv = lax.optimization_barrier((moving, back, dq, dk, dv))
    out_down, gate_up = moving
    if swap:
        output = swap_out(own, back[0], side)
    else:
        output = own.reshape(seqs, rows, D)
    diagonals = jnp.sum(jnp.concatenate(strips, axis=1), axis=0).reshape(HEADS, -1)
    table = jnp.dot(diagonals, one_hot, precision=PRECISE).T
    table = jnp.pad(table.reshape(1, -1), ((0, 0), (0, D - BUCKETS * HEADS)))
    dq = after(dq, output, table)
    dw, gain_one = finish_weights(x, gain_rows[0:1], wqkv, dq, dk, dv, tile)
    scatter_qk = scatter(dw)
    moving = next(scatter_qk)
    moving, dq = lax.optimization_barrier((moving, dq))
    moving = scatter_qk.send(moving)
    small = total(jnp.concatenate([gain_one, gain_two, table]))
    own, away_grad = finish_inputs(x, grad_hidden, wqkv, gain_rows[0:1], dq, dk, dv, place, tile, away)
    moving, small, own, away_grad = lax.optimization_barrier((moving, small, own, away_grad))
    back = [lax.ppermute(away_grad, "fsdp", [(0, 1), (1, 0)])] if swap else []
    moving = scatter_qk.send(moving)
    query_key = scatter_qk.send(moving)
    gain_shares = lax.dynamic_slice_in_dim(small[:2], lax.axis_index(BOTH) * gain_attn.shape[0], gain_attn.shape[0], 1)
    if swap:
        grad_inputs = swap_out(own, jnp.concatenate(back), side)
    else:
        grad_inputs = own.reshape(seqs, rows, D)
    return (
        output,
        grad_inputs,
        query_key[:, :D].T,
        query_key[:, D : 2 * D].T,
        query_key[:, 2 * D : 3 * D].T,
        out_down[:, :D].T,
        gate_up[:, :D].T,
        gate_up[:, D:].T,
        out_down[:, D:].T,
        gain_shares[0],
        gain_shares[1],
        small[2, : BUCKETS * HEADS].reshape(BUCKETS, HEADS),
    )


def solution(mesh):
    tokens = P("dp", "fsdp", None)
    columns = P(None, BOTH)
    return jax.shard_map(
        functools.partial(per_device, dict(mesh.shape)),
        mesh=mesh,
        in_specs=(tokens, tokens, P("dp")) + (columns,) * 7 + (P(BOTH), P(BOTH), P()),
        out_specs=(tokens, tokens) + (columns,) * 7 + (P(BOTH), P(BOTH), P()),
        check_vma=False,
    )
```
